128 devices in a mesh: dp: 4 (over x_lo, core), ctx: 32 (over z, y, x_hi).
Axes of the slice: x: 4 (x_hi: 2, x_lo: 2; x = x_hi * 2 + x_lo), y: 4, z: 4, core: 2. Of those that a mesh axis runs over, the one named last changes fastest.
Arguments:
- queries: bfloat16 [32768, 4096], P(('dp', 'ctx')), may hold values from -6 to 6
- keys: bfloat16 [32768, 512], P(('dp', 'ctx')), may hold values from -6 to 6
- values: bfloat16 [32768, 512], P(('dp', 'ctx')), may hold values from -6 to 6
- d_out: bfloat16 [4, 8192, 4096], P('dp', 'ctx'), may hold values from -6 to 6
- doc_ids: int32 [4, 8192], P('dp'), may hold values from 0 to 15, never falling along the last dimension, each value on 1 to 1024 neighbouring positions
- send_order: int32 [128, 256], P(('dp', 'ctx')), may hold values from 0 to 255, each once within a row
- place: int32 [128, 256], P(('dp', 'ctx')), may hold values from 0 to 255, each once within a row
Outputs:
- attended: bfloat16 [4, 8192, 4096], P('dp', 'ctx')
- grad_queries: bfloat16 [4, 8192, 4096], P('dp', 'ctx')
- grad_keys: bfloat16 [4, 8192, 512], P('dp', 'ctx')
- grad_values: bfloat16 [4, 8192, 512], P('dp', 'ctx')
The draws below stay inside these ranges and needn't reach their ends.
Inputs may be any that keep to these rules, and one draw needn't show every extreme that they name: `doc_ids`: within each sequence the numbers never fall, every number from 0 to 15 is used, each document holds 1 to 1024 positions and one holds exactly 1024. `send_order`: each row is a permutation of 0 to 255. `place`: each row is a permutation of 0 to 255.
All inputs are finite; a program needn't handle non-finite values.
Results may differ from the reference program's by a relative error of at most 0.04.
Values may be sent and summed in bfloat16 or wider, within the bound.
No kernel may reach another device: no remote copies, remote signals or barrier semaphores. Data moves between devices by JAX's collectives and lax.ppermute only.
A program may use at most 192 MiB of HBM per device.

```python
import math
import jax
import jax.numpy as jnp
import numpy as np
from jax import lax

HQ = 32
KEY_VALUE_HEADS = 4
HEAD_SIZE = 128
TOK_DEV = 256
LONGEST_DOC_LEN = 1024
SEQUENCE_LENGTH = 8192
TOKENS = 32768
GRAIN = 2
DOCS = 16
N_DP = 4
N_CTX = 32


def draw_queries(key, part):
    key = jax.random.fold_in(key, 11)
    first = jax.random.fold_in(key, 0)
    shape = (TOKENS, HQ * HEAD_SIZE)
    return jnp.clip(jax.random.normal(first, shape, jnp.float32), -6.0, 6.0).astype(jnp.bfloat16)


def draw_keys(key, part):
    key = jax.random.fold_in(key, 23)
    first = jax.random.fold_in(key, 0)
    shape = (TOKENS, KEY_VALUE_HEADS * HEAD_SIZE)
    return jnp.clip(jax.random.normal(first, shape, jnp.float32), -6.0, 6.0).astype(jnp.bfloat16)


def level_of(key, extent, cuts, least, high):
    def one(axis_at, parts):
        steps = jax.random.uniform(jax.random.fold_in(jax.random.fold_in(key, 6), axis_at), (parts,), jnp.float32, least / len(cuts), high / len(cuts))
        return jnp.repeat(jnp.exp(steps), extent[axis_at] // parts).reshape((-1,) + (1,) * (len(extent) - axis_at - 1))

    gain = one(*cuts[0])
    for cut in cuts[1:]:
        gain = gain * one(*cut)
    return gain


def profile(count, total, limit, slope):
    loads = [(1 << 20) // math.isqrt(standing ** slope) + 1 for standing in range(2, count + 1)]
    spare, holding = total - limit - (count - 1), [1] * (count - 1)
    while spare > 0:
        candidates = [i for i in range(count - 1) if holding[i] < limit]
        pool, remaining = sum([loads[i] for i in candidates]), spare
        for i in candidates:
            addition = min(limit - holding[i], max(1, remaining * loads[i] // pool), spare)
            holding[i] = holding[i] + addition
            spare = spare - addition
    return np.array([limit] + holding)


def ragged_sizes(rng, count, total, most, lean):
    if count == 2:
        one = jax.random.randint(rng, (), max(1, total - most), min(most, total - 1) + 1)
        return jnp.stack([one, total - one])
    lengths = jnp.asarray(profile(count, total, most, lean), jnp.int32)
    pairs = (count - 1) // 2
    donor, receiver = lengths[1:1 + 2 * pairs:2], lengths[2:2 + 2 * pairs:2]
    room = jnp.minimum(donor - 1, most - receiver)
    passed = jax.random.randint(jax.random.fold_in(rng, 1), (pairs,), 0, 1 << 20) % (room + 1)
    lengths = lengths.at[1:1 + 2 * pairs:2].set(donor - passed).at[2:2 + 2 * pairs:2].set(receiver + passed)
    return lengths[jax.random.permutation(jax.random.fold_in(rng, 2), count)]


def normal_values(stream_key, dims, deviation, most, shards=(), kind=jnp.bfloat16):
    array = deviation * jax.random.normal(stream_key, dims, jnp.float32)
    if shards:
        array = array * level_of(stream_key, dims, shards, -0.22, 0.18)
    return jnp.clip(array, -most, most).astype(kind)


def setup_inputs(seed: int = 0) -> dict:
    arg_keys = jax.random.split(jax.random.key(seed), 8)
    queries = draw_queries(jax.random.fold_in(arg_keys[7], 71), 0)
    keys = draw_keys(jax.random.fold_in(arg_keys[7], 71), 0)
    values = normal_values(arg_keys[2], (TOKENS, KEY_VALUE_HEADS * HEAD_SIZE), 1.0, 6.0, ((0, 128),))
    d_out = normal_values(arg_keys[3], (N_DP, SEQUENCE_LENGTH, HQ * HEAD_SIZE), 1.0, 6.0, ((0, 4), (1, 32)))
    doc_ids = jax.vmap(lambda own: jnp.searchsorted(jnp.cumsum(ragged_sizes(own, DOCS, SEQUENCE_LENGTH, LONGEST_DOC_LEN, 0)), jnp.arange(SEQUENCE_LENGTH), side="right"))(jax.random.split(arg_keys[4], N_DP)).reshape((N_DP, SEQUENCE_LENGTH)).astype(jnp.int32)
    send_order = jax.vmap(lambda own: jax.random.permutation(own, TOK_DEV))(jax.random.split(arg_keys[5], (N_DP * N_CTX))).reshape((N_DP * N_CTX, TOK_DEV)).astype(jnp.int32)
    place = jax.vmap(lambda own: jax.random.permutation(own, TOK_DEV))(jax.random.split(arg_keys[6], (N_DP * N_CTX))).reshape((N_DP * N_CTX, TOK_DEV)).astype(jnp.int32)
    return {"queries": queries, "keys": keys, "values": values, "d_out": d_out, "doc_ids": doc_ids, "send_order": send_order, "place": place}


def shard_pass(q_sh, do_sh, k_band, value_window, doc_q, doc_k, pos_q, pos_k):
    scale = 1.0 / math.sqrt(HEAD_SIZE)
    group = HQ // KEY_VALUE_HEADS
    q4 = q_sh.astype(jnp.float32).reshape(TOK_DEV, KEY_VALUE_HEADS, group, HEAD_SIZE)
    do4 = do_sh.astype(jnp.float32).reshape(TOK_DEV, KEY_VALUE_HEADS, group, HEAD_SIZE)
    kf = k_band.astype(jnp.float32)
    vf = value_window.astype(jnp.float32)
    keep = (doc_q[:, None] == doc_k[None, :]) & (pos_k[None, :] <= pos_q[:, None]) & (pos_k[None, :] >= 0)
    keep4 = keep[:, None, None, :]
    raw = jnp.einsum('tgrd,sgd->tgrs', q4, kf) * scale
    masked = jnp.where(keep4, raw, -jnp.inf)
    top = lax.optimization_barrier(jnp.max(masked, axis=-1))
    expo = jnp.where(keep4, jnp.exp(masked - top[..., None]), 0.0)
    total = lax.optimization_barrier(jnp.sum(expo, axis=-1))
    weights = expo.astype(jnp.bfloat16).astype(jnp.float32)
    mixed = jnp.einsum('tgrs,sgd->tgrd', weights, vf) / total[..., None]
    attended = mixed.astype(jnp.bfloat16)
    lse = top + jnp.log(total)
    delta = lax.optimization_barrier(jnp.sum(do4 * attended.astype(jnp.float32), axis=-1))
    probs = jnp.where(keep4, jnp.exp(masked - lse[..., None]), 0.0)
    probs_low = probs.astype(jnp.bfloat16).astype(jnp.float32)
    dv_band = jnp.einsum('tgrs,tgrd->sgd', probs_low, do4)
    dprob = jnp.einsum('tgrd,sgd->tgrs', do4, vf)
    dscore = (probs * (dprob - delta[..., None])).astype(jnp.bfloat16).astype(jnp.float32)
    dq = (jnp.einsum('tgrs,sgd->tgrd', dscore, kf) * scale).astype(jnp.bfloat16)
    dk_band = jnp.einsum('tgrs,tgrd->sgd', dscore, q4) * scale
    return (attended.reshape(TOK_DEV, HQ * HEAD_SIZE), dq.reshape(TOK_DEV, HQ * HEAD_SIZE), dk_band, dv_band)

def one_sequence(q_seq, k_seq, value_sequence, do_seq, doc_seq):
    token_window = LONGEST_DOC_LEN + TOK_DEV
    kpad = jnp.concatenate([jnp.zeros((LONGEST_DOC_LEN, KEY_VALUE_HEADS, HEAD_SIZE), jnp.bfloat16), k_seq.reshape(SEQUENCE_LENGTH, KEY_VALUE_HEADS, HEAD_SIZE)], axis=0)
    value_padded = jnp.concatenate([jnp.zeros((LONGEST_DOC_LEN, KEY_VALUE_HEADS, HEAD_SIZE), jnp.bfloat16), value_sequence.reshape(SEQUENCE_LENGTH, KEY_VALUE_HEADS, HEAD_SIZE)], axis=0)
    docpad = jnp.concatenate([jnp.full((LONGEST_DOC_LEN,), -1, jnp.int32), doc_seq.astype(jnp.int32)], axis=0)

    def step(carry, shard):
        dk_acc, dv_acc = carry
        window_begin = (shard * TOK_DEV).astype(jnp.int32)
        q_sh = lax.dynamic_slice_in_dim(q_seq, window_begin, TOK_DEV, 0)
        do_sh = lax.dynamic_slice_in_dim(do_seq, window_begin, TOK_DEV, 0)
        k_band = lax.dynamic_slice_in_dim(kpad, window_begin, token_window, 0)
        value_window = lax.dynamic_slice_in_dim(value_padded, window_begin, token_window, 0)
        doc_k = lax.dynamic_slice_in_dim(docpad, window_begin, token_window, 0)
        doc_q = lax.dynamic_slice_in_dim(doc_seq.astype(jnp.int32), window_begin, TOK_DEV, 0)
        pos_q = window_begin + jnp.arange(TOK_DEV, dtype=jnp.int32)
        pos_k = window_begin - LONGEST_DOC_LEN + jnp.arange(token_window, dtype=jnp.int32)
        attended, dq, dk_band, dv_band = shard_pass(q_sh, do_sh, k_band, value_window, doc_q, doc_k, pos_q, pos_k)
        dk_acc = lax.dynamic_update_slice_in_dim(dk_acc, lax.dynamic_slice_in_dim(dk_acc, window_begin, token_window, 0) + dk_band, window_begin, 0)
        dv_acc = lax.dynamic_update_slice_in_dim(dv_acc, lax.dynamic_slice_in_dim(dv_acc, window_begin, token_window, 0) + dv_band, window_begin, 0)
        return ((dk_acc, dv_acc), (attended, dq))
    zero_block = jnp.zeros((SEQUENCE_LENGTH + LONGEST_DOC_LEN, KEY_VALUE_HEADS, HEAD_SIZE), jnp.float32)
    (dk_acc, dv_acc), (attended, dq) = lax.scan(step, (zero_block, zero_block), jnp.arange(N_CTX, dtype=jnp.int32))
    grad_k = dk_acc[LONGEST_DOC_LEN:].reshape(SEQUENCE_LENGTH, KEY_VALUE_HEADS * HEAD_SIZE).astype(jnp.bfloat16)
    grad_v = dv_acc[LONGEST_DOC_LEN:].reshape(SEQUENCE_LENGTH, KEY_VALUE_HEADS * HEAD_SIZE).astype(jnp.bfloat16)
    return (attended.reshape(SEQUENCE_LENGTH, HQ * HEAD_SIZE), dq.reshape(SEQUENCE_LENGTH, HQ * HEAD_SIZE), grad_k, grad_v)

def reference(queries, keys, values, d_out, doc_ids, send_order, place):
    devices = N_DP * N_CTX
    source = jnp.arange(devices, dtype=jnp.int32)[:, None]
    column = jnp.arange(TOK_DEV, dtype=jnp.int32)[None, :]
    dest_dev = jnp.broadcast_to(column // GRAIN, (devices, TOK_DEV))
    arrival = source * GRAIN + column % GRAIN
    slot = place[dest_dev, arrival]
    target = (dest_dev * TOK_DEV + slot).reshape(-1)
    anchor = (source * TOK_DEV + send_order).reshape(-1)
    q_all = jnp.zeros_like(queries).at[target].set(queries[anchor]).reshape(N_DP, SEQUENCE_LENGTH, HQ * HEAD_SIZE)
    k_all = jnp.zeros_like(keys).at[target].set(keys[anchor]).reshape(N_DP, SEQUENCE_LENGTH, KEY_VALUE_HEADS * HEAD_SIZE)
    v_all = jnp.zeros_like(values).at[target].set(values[anchor]).reshape(N_DP, SEQUENCE_LENGTH, KEY_VALUE_HEADS * HEAD_SIZE)
    outs = [one_sequence(q_all[p], k_all[p], v_all[p], d_out[p], doc_ids[p]) for p in range(N_DP)]
    return (jnp.stack([o[0] for o in outs]), jnp.stack([o[1] for o in outs]), jnp.stack([o[2] for o in outs]), jnp.stack([o[3] for o in outs]))
```

```python
import functools
import math

import jax
import jax.numpy as jnp
from jax import lax
from jax.experimental import pallas as pl
from jax.experimental.pallas import tpu as pltpu
from jax.sharding import PartitionSpec as P

HQ = 32
KV_HEADS = 4
N_DP = 4
GROUP = HQ // KV_HEADS
HEAD = 128
SPAN = 4
BLOCKS = SPAN + 1
QCOLS = GROUP * HEAD
KVCOLS = 2 * HEAD
COLS = QCOLS + BLOCKS * KVCOLS
CHUNKS = ((0, 2, (2,)), (2, 2, (1, 1)))
SCALE = 1.0 / math.sqrt(HEAD)
LOG2E = math.log2(math.e)
MASKED = -1e30
VMEM_LIMIT = 60 * 1024 * 1024


def dot(a, b):
    return jnp.dot(a, b, preferred_element_type=jnp.float32)


def shifted(block, distance):
    devices = range(lax.axis_size("ctx"))
    route = [(i - distance, i) for i in devices if i - distance in devices]
    return lax.ppermute(block, "ctx", route)


def pack_kernel(order_ref, q_ref, k_ref, v_ref, *rest):
    out_ref = rest[-1]
    tok = q_ref.shape[0]
    n, grain, _ = out_ref.shape
    order = jnp.broadcast_to(order_ref[...].astype(jnp.float32), (tok, tok)).T
    column = lax.broadcasted_iota(jnp.int32, (tok, tok), 1)
    onehot = (order.astype(jnp.int32) == column).astype(jnp.bfloat16)
    q = dot(onehot, q_ref[...]).astype(jnp.bfloat16)
    out_ref[:, :, :QCOLS] = q.reshape(n, grain, QCOLS)
    kv = jnp.concatenate([k_ref[...], v_ref[...]], axis=1)
    kv = dot(onehot, kv).astype(jnp.bfloat16).reshape(n, grain, KVCOLS)
    ctx = n // N_DP
    for t in range(BLOCKS):
        back = SPAN - t
        at = QCOLS + t * KVCOLS
        for p in range(N_DP):
            if back:
                none = jnp.zeros((back, grain, KVCOLS), jnp.bfloat16)
                out_ref[p * ctx : p * ctx + back, :, at : at + KVCOLS] = none
            out_ref[p * ctx + back : (p + 1) * ctx, :, at : at + KVCOLS] = kv[
                p * ctx : (p + 1) * ctx - back
            ]


def first_pack_kernel(order_ref, q_ref, k_ref, v_ref, doc_ref, place_ref, out_ref, doc_out, place_out):
    doc_out[...] = doc_ref[...]
    place_out[...] = place_ref[...]
    pack_kernel(order_ref, q_ref, k_ref, v_ref, out_ref)


def pack(order, queries, keys, values, first, count, later=()):
    tok = queries.shape[0]
    devices = lax.axis_size("dp") * lax.axis_size("ctx")
    grain = tok // devices
    whole = [pl.BlockSpec(a.shape, lambda h: (0, 0)) for a in later]
    out = pl.pallas_call(
        first_pack_kernel if later else pack_kernel,
        grid=(count,),
        in_specs=[
            pl.BlockSpec(order.shape, lambda h: (0, 0)),
            pl.BlockSpec((tok, QCOLS), lambda h: (0, first + h)),
            pl.BlockSpec((tok, HEAD), lambda h: (0, first + h)),
            pl.BlockSpec((tok, HEAD), lambda h: (0, first + h)),
        ]
        + whole,
        out_specs=[pl.BlockSpec((devices, grain, COLS), lambda h: (0, 0, h))] + whole,
        out_shape=[jax.ShapeDtypeStruct((devices, grain, count * COLS), jnp.bfloat16)]
        + [jax.ShapeDtypeStruct(a.shape, a.dtype) for a in later],
        compiler_params=pltpu.CompilerParams(vmem_limit_bytes=VMEM_LIMIT),
        name="pack",
    )(order, queries, keys, values, *later)
    return out if later else out[0]


def attend_kernel(
    start_ref, place_ref, rx_ref, do_ref, att_old, dq_old,
    att_ref, dq_ref, term0, term1, term2, term3, own_ref,
    bias, k_all, v_all, kt, vt, q_loc, s_buf, ds_buf, dk, dv, *slots,
):
    tok = q_loc.shape[0]
    window = BLOCKS * tok
    slots = (slots[:4], slots[4:])

    @pl.when(pl.program_id(0) == 0)
    def _():
        u = lax.broadcasted_iota(jnp.int32, (window, tok), 0)
        t = lax.broadcasted_iota(jnp.int32, (window, tok), 1)
        keep = (u >= start_ref[...]) & (u <= t + SPAN * tok)
        bias[...] = jnp.where(keep, 0.0, MASKED)

    row = lax.broadcasted_iota(jnp.int32, (tok, tok), 0)
    rx = rx_ref[...].reshape(tok, COLS)
    for t in range(BLOCKS):
        spread = (place_ref[t : t + 1, :] == row).astype(jnp.bfloat16)
        at = QCOLS + t * KVCOLS
        kv = dot(spread, rx[:, at : at + KVCOLS])
        here = slice(t * tok, (t + 1) * tok)
        k_all[here, :] = kv[:, :HEAD].astype(jnp.bfloat16)
        v_all[here, :] = kv[:, HEAD:].astype(jnp.bfloat16)
        kt[:, here] = kv[:, :HEAD].T.astype(jnp.bfloat16)
        vt[:, here] = kv[:, HEAD:].T.astype(jnp.bfloat16)
        if t == SPAN:
            q_loc[...] = dot(spread, rx[:, :QCOLS]).astype(jnp.bfloat16)
    dk[...] = jnp.zeros_like(dk)
    dv[...] = jnp.zeros_like(dv)

    def tile(t):
        return slice(t * tok, (t + 1) * tok)

    def forward(r, slot):
        p_buf, dot_s, do_s, delta = slots[slot]
        cols = slice(r * HEAD, (r + 1) * HEAD)
        qt = q_loc[:, cols].T
        top = jnp.full((1, tok), MASKED, jnp.float32)
        for t in range(BLOCKS):
            s = dot(k_all[tile(t), :], qt) * (SCALE * LOG2E) + bias[tile(t), :]
            s_buf[tile(t), :] = s
            top = jnp.maximum(top, jnp.max(s, axis=0, keepdims=True))
            yield
        total = jnp.zeros((1, tok), jnp.float32)
        acc = None
        for t in range(BLOCKS):
            p = jnp.exp2(s_buf[tile(t), :] - top)
            total = total + jnp.sum(p, axis=0, keepdims=True)
            pb = p.astype(jnp.bfloat16)
            p_buf[tile(t), :] = pb
            part = dot(vt[:, tile(t)], pb)
            acc = part if acc is None else acc + part
            yield
        inv = 1.0 / total
        att = (acc * inv).astype(jnp.bfloat16)
        att_ref[:, cols] = att.T
        scaled = (do_ref[:, cols].T.astype(jnp.float32) * inv).astype(jnp.bfloat16)
        dot_s[...] = scaled
        do_s[...] = scaled.T
        delta[...] = jnp.sum(
            scaled.astype(jnp.float32) * att.astype(jnp.float32), axis=0, keepdims=True
        )
        yield

    def backward(r, slot):
        p_buf, dot_s, do_s, delta = slots[slot]
        cols = slice(r * HEAD, (r + 1) * HEAD)
        for t in range(BLOCKS):
            p = p_buf[tile(t), :]
            dp = dot(v_all[tile(t), :], dot_s[...])
            ds = (p.astype(jnp.float32) * (dp - delta[...])).astype(jnp.bfloat16)
            ds_buf[tile(t), :] = ds
            yield
            dv[tile(t), :] += dot(p, do_s[...])
            dk[tile(t), :] += dot(ds, q_loc[:, cols])
            yield
        dq = dot(kt[...], ds_buf[...]) * SCALE
        dq_ref[:, cols] = dq.T.astype(jnp.bfloat16)
        yield

    def together(*work):
        work = list(work)
        while work:
            work = [w for w in work if next(w, work) is None]

    together(forward(0, 0))
    for r in range(1, GROUP):
        together(forward(r, r % 2), backward(r - 1, (r - 1) % 2))
    together(backward(GROUP - 1, (GROUP - 1) % 2))
    for t, term in enumerate((term0, term1, term2, term3)):
        term[:, :HEAD] = (dk[tile(t), :] * SCALE).astype(jnp.bfloat16)
        term[:, HEAD:] = dv[tile(t), :].astype(jnp.bfloat16)
    own_ref[:, :HEAD] = dk[SPAN * tok :, :] * SCALE
    own_ref[:, HEAD:] = dv[SPAN * tok :, :]


def attend(start, places, rx, do, att, dq, first, count, at=0):
    tok = do.shape[0]
    window = BLOCKS * tok
    bf16, f32 = jnp.bfloat16, jnp.float32
    wide = pl.BlockSpec((tok, QCOLS), lambda h: (0, first + h))
    olds = () if att is None else (att, dq)
    body = attend_kernel
    if att is None:

        def body(a, b, c, d, *rest):
            attend_kernel(a, b, c, d, None, None, *rest)

    return pl.pallas_call(
        body,
        grid=(count,),
        in_specs=[
            pl.BlockSpec(start.shape, lambda h: (0, 0)),
            pl.BlockSpec(places.shape, lambda h: (0, 0)),
            pl.BlockSpec((*rx.shape[:2], COLS), lambda h: (0, 0, at + h)),
            wide,
        ]
        + [pl.BlockSpec(memory_space=pl.ANY)] * len(olds),
        out_specs=[
            wide,
            wide,
            *[pl.BlockSpec((tok, KVCOLS), lambda h: (0, h))] * BLOCKS,
        ],
        out_shape=[
            jax.ShapeDtypeStruct((tok, HQ * HEAD), bf16),
            jax.ShapeDtypeStruct((tok, HQ * HEAD), bf16),
            *[jax.ShapeDtypeStruct((tok, count * KVCOLS), bf16)] * SPAN,
            jax.ShapeDtypeStruct((tok, count * KVCOLS), f32),
        ],
        scratch_shapes=[
            pltpu.VMEM((window, tok), f32),
            pltpu.VMEM((window, HEAD), bf16),
            pltpu.VMEM((window, HEAD), bf16),
            pltpu.VMEM((HEAD, window), bf16),
            pltpu.VMEM((HEAD, window), bf16),
            pltpu.VMEM((tok, QCOLS), bf16),
            pltpu.VMEM((window, tok), f32),
            pltpu.VMEM((window, tok), bf16),
            pltpu.VMEM((window, HEAD), f32),
            pltpu.VMEM((window, HEAD), f32),
        ]
        + [
            pltpu.VMEM((window, tok), bf16),
            pltpu.VMEM((HEAD, tok), bf16),
            pltpu.VMEM((tok, HEAD), bf16),
            pltpu.VMEM((1, tok), f32),
        ]
        * 2,
        input_output_aliases={4: 0, 5: 1} if olds else {},
        compiler_params=pltpu.CompilerParams(vmem_limit_bytes=VMEM_LIMIT),
        cost_estimate=pl.CostEstimate(
            flops=count * GROUP * 48 * window * tok * HEAD,
            bytes_accessed=count * 4 * 1024 * 1024,
            transcendentals=count * GROUP * window * tok,
        ),
        name="attend",
    )(start, places, rx, do, *olds)


def finish_kernel(own_ref, b0, b1, b2, b3, *rest):
    gk_ref, gv_ref = rest[-2:]
    total = own_ref[...]
    for back in (b0, b1, b2, b3):
        total = total + back[...].astype(jnp.float32)
    gk_ref[...] = total[:, :HEAD].astype(jnp.bfloat16)
    gv_ref[...] = total[:, HEAD:].astype(jnp.bfloat16)


def finish(own, backs, olds, first, count):
    tok = own.shape[0]
    mine = pl.BlockSpec((tok, KVCOLS), lambda h: (0, h))
    return pl.pallas_call(
        finish_kernel,
        grid=(count,),
        in_specs=[mine] * BLOCKS + [pl.BlockSpec(memory_space=pl.ANY)] * len(olds),
        out_specs=[pl.BlockSpec((tok, HEAD), lambda h: (0, first + h))] * 2,
        out_shape=[jax.ShapeDtypeStruct((tok, KV_HEADS * HEAD), jnp.bfloat16)] * 2,
        input_output_aliases={BLOCKS: 0, BLOCKS + 1: 1} if olds else {},
        compiler_params=pltpu.CompilerParams(vmem_limit_bytes=VMEM_LIMIT),
        name="finish",
    )(own, *backs, *olds)


def body(queries, keys, values, d_out, doc_ids, send_order, place):
    tok = queries.shape[0]
    shard = lax.axis_index("ctx")
    sent = []
    for first, count, _ in CHUNKS:
        if first == 0:
            later = (doc_ids, place)
            packed, doc_ids, place = pack(send_order, queries, keys, values, first, count, later)
        else:
            packed = pack(send_order, queries, keys, values, first, count)
        sent.append(lax.all_to_all(packed, ("dp", "ctx"), split_axis=0, concat_axis=0, tiled=True))

    places = jnp.concatenate([shifted(place, SPAN - t) for t in range(SPAN)] + [place], axis=0)
    docs = jnp.pad(doc_ids[0], (SPAN * tok, 0), constant_values=-1)
    docs = lax.dynamic_slice_in_dim(docs, shard * tok, BLOCKS * tok, 0)
    before = docs[:, None] < docs[None, SPAN * tok :]
    start = jnp.sum(before.astype(jnp.int32), axis=0)[None, :]

    att = dq = None
    parts = []
    for (first, _, calls), rx in zip(CHUNKS, sent):
        at = 0
        for count in calls:
            out = attend(start, places, rx, d_out[0], att, dq, first + at, count, at)
            att, dq, *terms, own = out
            backs = [shifted(terms[t], t - SPAN) for t in range(SPAN)]
            parts.append((own, backs, first + at, count))
            at += count
    grads = ()
    for own, backs, first, count in parts:
        grads = finish(own, backs, grads, first, count)
    return att[None], dq[None], grads[0][None], grads[1][None]


def solution(mesh):
    in_specs = (
        P(("dp", "ctx"), None),
        P(("dp", "ctx"), None),
        P(("dp", "ctx"), None),
        P("dp", "ctx", None),
        P("dp", None),
        P(("dp", "ctx"), None),
        P(("dp", "ctx"), None),
    )
    out_specs = (P("dp", "ctx", None),) * 4
    return jax.shard_map(body, mesh=mesh, in_specs=in_specs, out_specs=out_specs, check_vma=False)
```

```python
import functools
import math

import jax
import jax.numpy as jnp
from jax import lax
from jax.experimental import pallas as pl
from jax.experimental.pallas import tpu as pltpu
from jax.sharding import PartitionSpec as P

HQ = 32
KV_HEADS = 4
N_DP = 4
GROUP = HQ // KV_HEADS
HEAD = 128
SPAN = 4
BLOCKS = SPAN + 1
QCOLS = GROUP * HEAD
KVCOLS = 2 * HEAD
COLS = QCOLS + BLOCKS * KVCOLS
FSTEP = 512
BSTEP = 400
CHUNKS = ((0, 2), (2, 2))
SCALE = 1.0 / math.sqrt(HEAD)
LOG2E = math.log2(math.e)
MASKED = -1e30
VMEM_LIMIT = 60 * 1024 * 1024
ATTEND_LIMIT = 32 * 1024 * 1024
SMALL_LIMIT = 8 * 1024 * 1024


def dot(a, b):
    return jnp.dot(a, b, preferred_element_type=jnp.float32)


def shifted(block, distance):
    devices = range(lax.axis_size("ctx"))
    route = [(i - distance, i) for i in devices if i - distance in devices]
    return lax.ppermute(block, "ctx", route)


def pack_kernel(order_ref, q_ref, k_ref, v_ref, *rest):
    out_ref = rest[-1]
    tok = q_ref.shape[0]
    n, grain, _ = out_ref.shape
    order = jnp.broadcast_to(order_ref[...].astype(jnp.float32), (tok, tok)).T
    column = lax.broadcasted_iota(jnp.int32, (tok, tok), 1)
    onehot = (order.astype(jnp.int32) == column).astype(jnp.bfloat16)
    q = dot(onehot, q_ref[...]).astype(jnp.bfloat16)
    out_ref[:, :, :QCOLS] = q.reshape(n, grain, QCOLS)
    kv = jnp.concatenate([k_ref[...], v_ref[...]], axis=1)
    kv = dot(onehot, kv).astype(jnp.bfloat16).reshape(n, grain, KVCOLS)
    ctx = n // N_DP
    for t in range(BLOCKS):
        back = SPAN - t
        at = QCOLS + t * KVCOLS
        for p in range(N_DP):
            if back:
                none = jnp.zeros((back, grain, KVCOLS), jnp.bfloat16)
                out_ref[p * ctx : p * ctx + back, :, at : at + KVCOLS] = none
            out_ref[p * ctx + back : (p + 1) * ctx, :, at : at + KVCOLS] = kv[
                p * ctx : (p + 1) * ctx - back
            ]


def first_pack_kernel(order_ref, q_ref, k_ref, v_ref, doc_ref, place_ref, out_ref, doc_out, place_out):
    doc_out[...] = doc_ref[...]
    place_out[...] = place_ref[...]
    pack_kernel(order_ref, q_ref, k_ref, v_ref, out_ref)


def pack(order, queries, keys, values, first, count, later=()):
    tok = queries.shape[0]
    devices = lax.axis_size("dp") * lax.axis_size("ctx")
    grain = tok // devices
    whole = [pl.BlockSpec(a.shape, lambda h: (0, 0)) for a in later]
    out = pl.pallas_call(
        first_pack_kernel if later else pack_kernel,
        grid=(count,),
        in_specs=[
            pl.BlockSpec(order.shape, lambda h: (0, 0)),
            pl.BlockSpec((tok, QCOLS), lambda h: (0, first + h)),
            pl.BlockSpec((tok, HEAD), lambda h: (0, first + h)),
            pl.BlockSpec((tok, HEAD), lambda h: (0, first + h)),
        ]
        + whole,
        out_specs=[pl.BlockSpec((devices, grain, COLS), lambda h: (0, 0, h))] + whole,
        out_shape=[jax.ShapeDtypeStruct((devices, grain, count * COLS), jnp.bfloat16)]
        + [jax.ShapeDtypeStruct(a.shape, a.dtype) for a in later],
        compiler_params=pltpu.CompilerParams(vmem_limit_bytes=VMEM_LIMIT),
        name="pack",
    )(order, queries, keys, values, *later)
    return out if later else out[0]


def tiles(half, low, high, tok, step, cut=None):
    low = max(low, half * tok // 2)
    high = min(high, SPAN * tok + (half + 1) * tok // 2)
    for low, high in ((low, high),) if cut is None else ((low, cut), (cut, high)):
        size = (high - low) // pl.cdiv(high - low, step)
        for i in range(low, high, size):
            yield slice(i, i + size)


def moved(here, base):
    return slice(here.start - base, here.stop - base)


def together(*work):
    work = list(work)
    while work:
        work = [w for w in work if next(w, work) is None]


def halves(unit, tok):
    half, pair = unit % 2, unit // 2
    rows = slice(half * tok // 2, (half + 1) * tok // 2)
    one, two = ((2 * pair + i) * HEAD for i in range(2))
    return half, rows, slice(one, one + HEAD), slice(two, two + HEAD)


def backward(half, low, high, p_of, ds_buf, q, do_s, dot_s, delta, k_all, v_all, kt, dk, dv, base, done):
    tok = q.shape[0]
    spans = list(tiles(half, low, high, tok, BSTEP))
    for here in spans:
        p = p_of(here)
        dp = dot(v_all[moved(here, base), :], dot_s[...])
        ds = (p.astype(jnp.float32) * (dp - delta[...])).astype(jnp.bfloat16)
        ds_buf[moved(here, spans[0].start), :] = ds
        yield
        dv[moved(here, base), :] += dot(p, do_s[...])
        dk[moved(here, base), :] += dot(ds, q[...])
        yield
    first, last = spans[0].start, spans[-1].stop
    done(dot(kt[:, first - base : last - base], ds_buf[: last - first, :]))
    yield


def store_heads(ref, value, rows, one, two):
    half = value.shape[0] // 2
    ref[rows, one] = value[:half]
    ref[rows, two] = value[half:]


def attend_body(
    cut, start_ref, place_ref, rx_ref, do_ref, att_ref, bias, k_all, v_all, kt, vt,
    q_loc, s_buf, ds_buf, dk, dv, p_of, saved, done, stop,
):
    tok = q_loc.shape[0]
    window = BLOCKS * tok
    reach = SPAN * tok + tok // 2

    @pl.when(pl.program_id(0) == 0)
    def _():
        u = lax.broadcasted_iota(jnp.int32, (reach, tok // 2), 0)
        t = lax.broadcasted_iota(jnp.int32, (reach, tok // 2), 1)
        for half in range(2):
            off = half * tok // 2
            start = start_ref[:, off : off + tok // 2] - off
            keep = (u >= start) & (u <= t + SPAN * tok)
            add = jnp.where(keep, 0.0, MASKED)
            bias[half, :, : tok // 2] = add
            bias[half, :, tok // 2 :] = add

    row = lax.broadcasted_iota(jnp.int32, (tok, tok), 0)
    rx = rx_ref[...].reshape(tok, COLS)
    for t in range(BLOCKS):
        spread = (place_ref[t : t + 1, :] == row).astype(jnp.bfloat16)
        at = QCOLS + t * KVCOLS
        kv = dot(spread, rx[:, at : at + KVCOLS])
        here = slice(t * tok, (t + 1) * tok)
        k_all[here, :] = kv[:, :HEAD].astype(jnp.bfloat16)
        v_all[here, :] = kv[:, HEAD:].astype(jnp.bfloat16)
        kt[:, here] = kv[:, :HEAD].T.astype(jnp.bfloat16)
        vt[:, here] = kv[:, HEAD:].T.astype(jnp.bfloat16)
        if t == SPAN:
            q_loc[...] = dot(spread, rx[:, :QCOLS]).astype(jnp.bfloat16)
    dk[...] = jnp.zeros_like(dk)
    dv[...] = jnp.zeros_like(dv)

    def forward(unit):
        half, rows, one, two = halves(unit, tok)
        off = half * tok // 2
        q_u, do_s, dot_s, delta = saved(unit)
        q = jnp.concatenate([q_loc[rows, one], q_loc[rows, two]], axis=0)
        q_u[...] = q
        qt = q.T
        top = jnp.full((1, tok), MASKED, jnp.float32)
        for here in tiles(half, 0, window, tok, FSTEP, cut):
            s = dot(k_all[here, :], qt) * (SCALE * LOG2E) + bias[half, moved(here, off), :]
            s_buf[moved(here, off), :] = s
            top = jnp.maximum(top, jnp.max(s, axis=0, keepdims=True))
            yield
        total = jnp.zeros((1, tok), jnp.float32)
        acc = None
        for here in tiles(half, 0, window, tok, FSTEP, cut):
            p = jnp.exp2(s_buf[moved(here, off), :] - top)
            total = total + jnp.sum(p, axis=0, keepdims=True)
            low = p.astype(jnp.bfloat16)
            p_of(unit, here)[...] = low
            part = dot(vt[:, here], low)
            acc = part if acc is None else acc + part
            yield
        inv = 1.0 / total
        att = (acc * inv).astype(jnp.bfloat16)
        store_heads(att_ref, att.T, rows, one, two)
        do = jnp.concatenate([do_ref[rows, one], do_ref[rows, two]], axis=0)
        scaled = (do.T.astype(jnp.float32) * inv).astype(jnp.bfloat16)
        dot_s[...] = scaled
        do_s[...] = scaled.T
        delta[...] = jnp.sum(
            scaled.astype(jnp.float32) * att.astype(jnp.float32), axis=0, keepdims=True
        )
        yield

    def back(unit):
        return backward(
            unit % 2, 0, stop, lambda here: p_of(unit, here)[...], ds_buf, *saved(unit),
            k_all, v_all, kt, dk, dv, 0, lambda dq: done(unit, dq),
        )

    together(forward(0))
    for unit in range(1, GROUP):
        together(forward(unit), back(unit - 1))
    together(back(GROUP - 1))


def store_terms(terms, dk, dv, tok, base=0):
    for t, term in enumerate(terms):
        here = slice(t * tok - base, (t + 1) * tok - base)
        term[:, :HEAD] = (dk[here, :] * SCALE).astype(term.dtype)
        term[:, HEAD:] = dv[here, :].astype(term.dtype)


def attend_kernel(*refs):
    start_ref, place_ref, rx_ref, do_ref, att_ref, dq_ref, far, near2, near1, own = refs[:10]
    bias, k_all, v_all, kt, vt, q_loc, s_buf, ds_buf, dk, dv = refs[10:20]
    slots = (refs[20:25], refs[25:30])
    tok = q_loc.shape[0]

    def p_of(unit, here):
        p_buf = slots[unit % 2][0]
        return p_buf.at[moved(here, unit % 2 * tok // 2), :]

    def saved(unit):
        return slots[unit % 2][1:]

    def done(unit, dq):
        _, rows, one, two = halves(unit, tok)
        store_heads(dq_ref, (dq * SCALE).T.astype(jnp.bfloat16), rows, one, two)

    attend_body(
        None, start_ref, place_ref, rx_ref, do_ref, att_ref, bias, k_all, v_all, kt, vt,
        q_loc, s_buf, ds_buf, dk, dv, p_of, saved, done, BLOCKS * tok,
    )
    store_terms((far.at[0], far.at[1], near2, near1, own), dk, dv, tok)


def scratch(tok):
    window, reach = BLOCKS * tok, SPAN * tok + tok // 2
    bf16, f32 = jnp.bfloat16, jnp.float32
    return [
        pltpu.VMEM((2, reach, tok), f32),
        pltpu.VMEM((window, HEAD), bf16),
        pltpu.VMEM((window, HEAD), bf16),
        pltpu.VMEM((HEAD, window), bf16),
        pltpu.VMEM((HEAD, window), bf16),
        pltpu.VMEM((tok, QCOLS), bf16),
        pltpu.VMEM((reach, tok), f32),
        pltpu.VMEM((reach, tok), bf16),
        pltpu.VMEM((window, HEAD), f32),
        pltpu.VMEM((window, HEAD), f32),
    ]


def kept(tok):
    bf16 = jnp.bfloat16
    return [
        ((tok, HEAD), bf16),
        ((tok, HEAD), bf16),
        ((HEAD, tok), bf16),
        ((1, tok), jnp.float32),
    ]


def estimate(count, share, tok):
    work = count * GROUP * BLOCKS * tok * tok
    return pl.CostEstimate(
        flops=int(share * 48 * work * HEAD),
        bytes_accessed=count * 4 * 1024 * 1024,
        transcendentals=work,
    )


def attend(start, places, rx, do, first, count, at=0):
    tok = do.shape[0]
    bf16, f32 = jnp.bfloat16, jnp.float32
    wide = pl.BlockSpec((tok, QCOLS), lambda h: (0, first + h))
    cols = pl.BlockSpec((tok, KVCOLS), lambda h: (0, h))
    slot = [pltpu.VMEM((SPAN * tok + tok // 2, tok), bf16)]
    slot += [pltpu.VMEM(*a) for a in kept(tok)]
    return pl.pallas_call(
        attend_kernel,
        grid=(count,),
        in_specs=[
            pl.BlockSpec(start.shape, lambda h: (0, 0)),
            pl.BlockSpec(places.shape, lambda h: (0, 0)),
            pl.BlockSpec((*rx.shape[:2], COLS), lambda h: (0, 0, at + h)),
            wide,
        ],
        out_specs=[wide, wide, pl.BlockSpec((2, tok, KVCOLS), lambda h: (0, 0, h)), cols, cols, cols],
        out_shape=[
            jax.ShapeDtypeStruct((tok, HQ * HEAD), bf16),
            jax.ShapeDtypeStruct((tok, HQ * HEAD), bf16),
            jax.ShapeDtypeStruct((2, tok, count * KVCOLS), bf16),
            jax.ShapeDtypeStruct((tok, count * KVCOLS), bf16),
            jax.ShapeDtypeStruct((tok, count * KVCOLS), bf16),
            jax.ShapeDtypeStruct((tok, count * KVCOLS), f32),
        ],
        scratch_shapes=scratch(tok) + slot + slot,
        compiler_params=pltpu.CompilerParams(vmem_limit_bytes=ATTEND_LIMIT),
        cost_estimate=estimate(count, 1.0, tok),
        name="attend",
    )(start, places, rx, do)


def attend_far_kernel(*refs):
    start_ref, place_ref, rx_ref, do_ref = refs[:4]
    att_ref, far, p_out, q_out, do_out, dot_out, delta_out, dq_out = refs[-23:-15]
    k_out, v_out, kt_out = refs[-15:-12]
    bias, k_all, v_all, kt, vt, q_loc, s_buf, ds_buf, dk, dv = refs[-12:-2]
    p_bufs = refs[-2:]
    tok = q_loc.shape[0]
    split = 2 * tok

    def p_of(unit, here):
        if here.start >= split:
            return p_out.at[unit, moved(here, split), :]
        return p_bufs[unit % 2].at[moved(here, unit % 2 * tok // 2), :]

    def saved(unit):
        return q_out.at[unit], do_out.at[unit], dot_out.at[unit], delta_out.at[unit]

    def done(unit, dq):
        dq_out[unit, :, :] = dq

    attend_body(
        split, start_ref, place_ref, rx_ref, do_ref, att_ref, bias, k_all, v_all, kt, vt,
        q_loc, s_buf, ds_buf, dk, dv, p_of, saved, done, split,
    )
    k_out[...] = k_all[split:, :]
    v_out[...] = v_all[split:, :]
    kt_out[...] = kt[:, split:]
    store_terms((far.at[0], far.at[1]), dk, dv, tok)


def attend_far(start, places, rx, do, old, first, at, after=()):
    tok = do.shape[0]
    count = rx.shape[2] // COLS
    near = BLOCKS * tok - 2 * tok
    bf16, f32 = jnp.bfloat16, jnp.float32
    wide = pl.BlockSpec((tok, QCOLS), lambda h: (0, first + at))
    state = [((near, tok), bf16)] + kept(tok) + [((HEAD, tok), f32)]
    state = [((GROUP, *shape), dtype) for shape, dtype in state]
    state += [((near, HEAD), bf16), ((near, HEAD), bf16), ((HEAD, near), bf16)]
    out = pl.pallas_call(
        attend_far_kernel,
        grid=(1,),
        in_specs=[
            pl.BlockSpec(start.shape, lambda h: (0, 0)),
            pl.BlockSpec(places.shape, lambda h: (0, 0)),
            pl.BlockSpec((*rx.shape[:2], COLS), lambda h: (0, 0, at)),
            wide,
        ]
        + [pl.BlockSpec(memory_space=pl.ANY)] * (len(old) + len(after)),
        out_specs=[wide, pl.BlockSpec((2, tok, KVCOLS), lambda h: (0, 0, at))]
        + [per_head(shape, at) for shape, _ in state],
        out_shape=[
            jax.ShapeDtypeStruct((tok, HQ * HEAD), bf16),
            jax.ShapeDtypeStruct((2, tok, count * KVCOLS), bf16),
        ]
        + [jax.ShapeDtypeStruct((count, *shape), dtype) for shape, dtype in state],
        scratch_shapes=scratch(tok) + [pltpu.VMEM((SPAN * tok + tok // 2, tok), bf16)] * 2,
        input_output_aliases={4 + i: i for i in range(len(old))},
        compiler_params=pltpu.CompilerParams(vmem_limit_bytes=ATTEND_LIMIT),
        cost_estimate=estimate(1, 0.6, tok),
        name="attend_far",
    )(start, places, rx, do, *old, *after)
    return out


def per_head(shape, at=None):
    zeros = [0] * len(shape)
    return pl.BlockSpec((None, *shape), lambda h: (h if at is None else at, *zeros))


def attend_near_kernel(*refs):
    p_in, q_in, do_in, dot_in, delta_in, dq_in, k_in, v_in, kt_in = refs[:9]
    dq_ref, near2, near1, own, dk, dv = refs[-8:-2]
    ds_bufs = refs[-2:]
    tok = near2.shape[0]
    split = 2 * tok
    dk[...] = jnp.zeros_like(dk)
    dv[...] = jnp.zeros_like(dv)

    def back(unit):
        def done(dq):
            _, rows, one, two = halves(unit, tok)
            dq = ((dq + dq_in[unit]) * SCALE).T.astype(jnp.bfloat16)
            store_heads(dq_ref, dq, rows, one, two)

        return backward(
            unit % 2, split, BLOCKS * tok, lambda here: p_in[unit, moved(here, split), :],
            ds_bufs[unit % 2], q_in.at[unit], do_in.at[unit], dot_in.at[unit],
            delta_in.at[unit], k_in, v_in, kt_in, dk, dv, split, done,
        )

    for unit in range(0, GROUP, 2):
        together(back(unit), back(unit + 1))
    store_terms((near2, near1, own), dk, dv, tok)


def attend_near(state, dq, first, count, after):
    tok = dq.shape[0]
    near = BLOCKS * tok - 2 * tok
    bf16, f32 = jnp.bfloat16, jnp.float32
    wide = pl.BlockSpec((tok, QCOLS), lambda h: (0, first + h))
    cols = pl.BlockSpec((tok, KVCOLS), lambda h: (0, h))
    return pl.pallas_call(
        attend_near_kernel,
        grid=(count,),
        in_specs=[per_head(a.shape[1:]) for a in state]
        + [pl.BlockSpec(memory_space=pl.ANY)] * (1 + len(after)),
        out_specs=[wide, cols, cols, cols],
        out_shape=[
            jax.ShapeDtypeStruct((tok, HQ * HEAD), bf16),
            jax.ShapeDtypeStruct((tok, count * KVCOLS), bf16),
            jax.ShapeDtypeStruct((tok, count * KVCOLS), bf16),
            jax.ShapeDtypeStruct((tok, count * KVCOLS), f32),
        ],
        scratch_shapes=[pltpu.VMEM((near, HEAD), f32)] * 2 + [pltpu.VMEM((near, tok), bf16)] * 2,
        input_output_aliases={len(state): 0},
        compiler_params=pltpu.CompilerParams(vmem_limit_bytes=ATTEND_LIMIT),
        cost_estimate=estimate(count, 0.4, tok),
        name="attend_near",
    )(*state, dq, *after)


def added(near, far):
    return (near[...].astype(jnp.float32) + far.astype(jnp.float32)).astype(jnp.bfloat16)


def merge_kernel(near2, near1, far, out2, out1):
    out2[...] = added(near2, far[0])
    out1[...] = added(near1, far[1])


def last_merge_kernel(near2, near1, far, own, back2, back1, out2, out1, total):
    merge_kernel(near2, near1, far, out2, out1)
    total[...] = own[...] + back2[...].astype(jnp.float32) + back1[...].astype(jnp.float32)


def merge(near2, near1, far, *own):
    shape = jax.ShapeDtypeStruct(near2.shape, jnp.bfloat16)
    total = [jax.ShapeDtypeStruct(a.shape, a.dtype) for a in own[:1]]
    return pl.pallas_call(
        last_merge_kernel if own else merge_kernel,
        out_shape=[shape, shape] + total,
        compiler_params=pltpu.CompilerParams(vmem_limit_bytes=SMALL_LIMIT),
        name="merge",
    )(near2, near1, far, *own)


def finish_kernel(done, own, back2, back1, gk_ref, gv_ref):
    width = own.shape[1]
    last = own[...] + back2[...].astype(jnp.float32) + back1[...].astype(jnp.float32)
    for at, total in ((0, done[...]), (width, last)):
        for i in range(width // KVCOLS):
            cols = slice((at // KVCOLS + i) * HEAD, (at // KVCOLS + i + 1) * HEAD)
            mid = i * KVCOLS + HEAD
            gk_ref[:, cols] = total[:, mid - HEAD : mid].astype(jnp.bfloat16)
            gv_ref[:, cols] = total[:, mid : mid + HEAD].astype(jnp.bfloat16)


def finish(*parts):
    tok = parts[0].shape[0]
    return pl.pallas_call(
        finish_kernel,
        out_shape=[jax.ShapeDtypeStruct((tok, KV_HEADS * HEAD), jnp.bfloat16)] * 2,
        compiler_params=pltpu.CompilerParams(vmem_limit_bytes=SMALL_LIMIT),
        name="finish",
    )(*parts)


def body(queries, keys, values, d_out, doc_ids, send_order, place):
    tok = queries.shape[0]
    shard = lax.axis_index("ctx")
    sent = []
    for first, count in CHUNKS:
        if first == 0:
            later = (doc_ids, place)
            packed, doc_ids, place = pack(send_order, queries, keys, values, first, count, later)
        else:
            packed = pack(send_order, queries, keys, values, first, count)
        sent.append(lax.all_to_all(packed, ("dp", "ctx"), split_axis=0, concat_axis=0, tiled=True))

    places = jnp.concatenate([shifted(place, SPAN - t) for t in range(SPAN)] + [place], axis=0)
    docs = jnp.pad(doc_ids[0], (SPAN * tok, 0), constant_values=-1)
    docs = lax.dynamic_slice_in_dim(docs, shard * tok, BLOCKS * tok, 0)
    before = docs[:, None] < docs[None, SPAN * tok :]
    start = jnp.sum(before.astype(jnp.int32), axis=0)[None, :]

    do = d_out[0]
    (first_a, count_a), (first_b, count_b) = CHUNKS
    att, dq, far_a, near2_a, near1_a, own_a = attend(start, places, sent[0], do, first_a, count_a)
    far_a = shifted(far_a, -2)
    half = attend_far(start, places, sent[1], do, (att,), first_b, 0)
    back2_a, back1_a = merge(near2_a, near1_a, far_a)
    after = (back1_a,)
    back2_a, back1_a = shifted(back2_a, -2), shifted(back1_a, -1)
    att, far_b, *state = attend_far(start, places, sent[1], do, half, first_b, 1, after)
    far_b = shifted(far_b, -2)
    dq, near2_b, near1_b, own_b = attend_near(state, dq, first_b, count_b, (back2_a, back1_a))
    back2_b, back1_b, total_a = merge(near2_b, near1_b, far_b, own_a, back2_a, back1_a)
    back2_b, back1_b = shifted(back2_b, -2), shifted(back1_b, -1)
    grad_k, grad_v = finish(total_a, own_b, back2_b, back1_b)
    return att[None], dq[None], grad_k[None], grad_v[None]


def solution(mesh):
    in_specs = (
        P(("dp", "ctx"), None),
        P(("dp", "ctx"), None),
        P(("dp", "ctx"), None),
        P("dp", "ctx", None),
        P("dp", None),
        P(("dp", "ctx"), None),
        P(("dp", "ctx"), None),
    )
    out_specs = (P("dp", "ctx", None),) * 4
    return jax.shard_map(body, mesh=mesh, in_specs=in_specs, out_specs=out_specs, check_vma=False)
```

```python
import functools
import math

import jax
import jax.numpy as jnp
from jax import lax
from jax.experimental import pallas as pl
from jax.experimental.pallas import tpu as pltpu
from jax.sharding import PartitionSpec as P

HQ = 32
KV_HEADS = 4
N_DP = 4
GROUP = HQ // KV_HEADS
HEAD = 128
SPAN = 4
BLOCKS = SPAN + 1
QCOLS = GROUP * HEAD
KVCOLS = 2 * HEAD
COLS = QCOLS + BLOCKS * KVCOLS
FSTEP = 512
BSTEP = 600
CHUNKS = ((0, 2), (2, 2))
SCALE = 1.0 / math.sqrt(HEAD)
LOG2E = math.log2(math.e)
MASKED = -1e30
VMEM_LIMIT = 60 * 1024 * 1024
ATTEND_LIMIT = 32 * 1024 * 1024
FAR_LIMIT = 32 * 1024 * 1024
SMALL_LIMIT = 8 * 1024 * 1024


def dot(a, b):
    return jnp.dot(a, b, preferred_element_type=jnp.float32)


def shifted(block, distance):
    devices = range(lax.axis_size("ctx"))
    route = [(i - distance, i) for i in devices if i - distance in devices]
    return lax.ppermute(block, "ctx", route)


def pack_kernel(order_ref, q_ref, k_ref, v_ref, *rest):
    out_ref = rest[-1]
    tok = q_ref.shape[0]
    n, grain, _ = out_ref.shape
    order = jnp.broadcast_to(order_ref[...].astype(jnp.float32), (tok, tok)).T
    column = lax.broadcasted_iota(jnp.int32, (tok, tok), 1)
    onehot = (order.astype(jnp.int32) == column).astype(jnp.bfloat16)
    q = dot(onehot, q_ref[...]).astype(jnp.bfloat16)
    out_ref[:, :, :QCOLS] = q.reshape(n, grain, QCOLS)
    kv = jnp.concatenate([k_ref[...], v_ref[...]], axis=1)
    kv = dot(onehot, kv).astype(jnp.bfloat16).reshape(n, grain, KVCOLS)
    ctx = n // N_DP
    for t in range(BLOCKS):
        back = SPAN - t
        at = QCOLS + t * KVCOLS
        for p in range(N_DP):
            if back:
                none = jnp.zeros((back, grain, KVCOLS), jnp.bfloat16)
                out_ref[p * ctx : p * ctx + back, :, at : at + KVCOLS] = none
            out_ref[p * ctx + back : (p + 1) * ctx, :, at : at + KVCOLS] = kv[
                p * ctx : (p + 1) * ctx - back
            ]


def first_pack_kernel(order_ref, q_ref, k_ref, v_ref, doc_ref, place_ref, out_ref, doc_out, place_out):
    doc_out[...] = doc_ref[...]
    place_out[...] = place_ref[...]
    pack_kernel(order_ref, q_ref, k_ref, v_ref, out_ref)


def pack(order, queries, keys, values, first, count, later=()):
    tok = queries.shape[0]
    devices = lax.axis_size("dp") * lax.axis_size("ctx")
    grain = tok // devices
    whole = [pl.BlockSpec(a.shape, lambda h: (0, 0)) for a in later]
    out = pl.pallas_call(
        first_pack_kernel if later else pack_kernel,
        grid=(count,),
        in_specs=[
            pl.BlockSpec(order.shape, lambda h: (0, 0)),
            pl.BlockSpec((tok, QCOLS), lambda h: (0, first + h)),
            pl.BlockSpec((tok, HEAD), lambda h: (0, first + h)),
            pl.BlockSpec((tok, HEAD), lambda h: (0, first + h)),
        ]
        + whole,
        out_specs=[pl.BlockSpec((devices, grain, COLS), lambda h: (0, 0, h))] + whole,
        out_shape=[jax.ShapeDtypeStruct((devices, grain, count * COLS), jnp.bfloat16)]
        + [jax.ShapeDtypeStruct(a.shape, a.dtype) for a in later],
        compiler_params=pltpu.CompilerParams(vmem_limit_bytes=VMEM_LIMIT),
        name="pack",
    )(order, queries, keys, values, *later)
    return out if later else out[0]


def tiles(half, low, high, tok, step, cut=None):
    low = max(low, half * tok // 2)
    high = min(high, SPAN * tok + (half + 1) * tok // 2)
    for low, high in ((low, high),) if cut is None else ((low, cut), (cut, high)):
        size = (high - low) // pl.cdiv(high - low, step)
        for i in range(low, high, size):
            yield slice(i, i + size)


def moved(here, base):
    return slice(here.start - base, here.stop - base)


def together(*work):
    work = list(work)
    while work:
        work = [w for w in work if next(w, work) is None]


def halves(unit, tok):
    half, pair = unit % 2, unit // 2
    rows = slice(half * tok // 2, (half + 1) * tok // 2)
    one, two = ((2 * pair + i) * HEAD for i in range(2))
    return half, rows, slice(one, one + HEAD), slice(two, two + HEAD)


def backward(half, low, high, p_of, ds_buf, q, do_s, dot_s, delta, k_all, v_all, kt, dk, dv, base, done):
    tok = q.shape[0]
    spans = list(tiles(half, low, high, tok, BSTEP))
    for here in spans:
        p = p_of(here)
        dp = dot(v_all[moved(here, base), :], dot_s[...])
        ds = (p.astype(jnp.float32) * (dp - delta[...])).astype(jnp.bfloat16)
        ds_buf[moved(here, spans[0].start), :] = ds
        yield
        dv[moved(here, base), :] += dot(p, do_s[...])
        dk[moved(here, base), :] += dot(ds, q[...])
        yield
    first, last = spans[0].start, spans[-1].stop
    done(dot(kt[:, first - base : last - base], ds_buf[: last - first, :]))
    yield


def store_heads(ref, value, rows, one, two):
    half = value.shape[0] // 2
    ref[rows, one] = value[:half]
    ref[rows, two] = value[half:]


def attend_body(
    cut, start_ref, place_ref, rx_ref, do_ref, att_ref, bias, k_all, v_all, kt, vt,
    q_loc, s_buf, ds_buf, dk, dv, p_of, saved, done, stop,
):
    tok = q_loc.shape[0]
    window = BLOCKS * tok
    reach = SPAN * tok + tok // 2

    @pl.when(pl.program_id(0) == 0)
    def _():
        u = lax.broadcasted_iota(jnp.int32, (reach, tok // 2), 0)
        t = lax.broadcasted_iota(jnp.int32, (reach, tok // 2), 1)
        for half in range(2):
            off = half * tok // 2
            start = start_ref[:, off : off + tok // 2] - off
            keep = (u >= start) & (u <= t + SPAN * tok)
            add = jnp.where(keep, 0.0, MASKED)
            bias[half, :, : tok // 2] = add
            bias[half, :, tok // 2 :] = add

    row = lax.broadcasted_iota(jnp.int32, (tok, tok), 0)
    rx = rx_ref[...].reshape(tok, COLS)
    for t in range(BLOCKS):
        spread = (place_ref[t : t + 1, :] == row).astype(jnp.bfloat16)
        at = QCOLS + t * KVCOLS
        kv = dot(spread, rx[:, at : at + KVCOLS])
        here = slice(t * tok, (t + 1) * tok)
        k_all[here, :] = kv[:, :HEAD].astype(jnp.bfloat16)
        v_all[here, :] = kv[:, HEAD:].astype(jnp.bfloat16)
        kt[:, here] = kv[:, :HEAD].T.astype(jnp.bfloat16)
        vt[:, here] = kv[:, HEAD:].T.astype(jnp.bfloat16)
        if t == SPAN:
            q_loc[...] = dot(spread, rx[:, :QCOLS]).astype(jnp.bfloat16)
    dk[...] = jnp.zeros_like(dk)
    dv[...] = jnp.zeros_like(dv)

    def forward(unit):
        half, rows, one, two = halves(unit, tok)
        off = half * tok // 2
        q_u, do_s, dot_s, delta = saved(unit)
        q = jnp.concatenate([q_loc[rows, one], q_loc[rows, two]], axis=0)
        q_u[...] = q
        qt = q.T
        top = jnp.full((1, tok), MASKED, jnp.float32)
        for here in tiles(half, 0, window, tok, FSTEP, cut):
            s = dot(k_all[here, :], qt) * (SCALE * LOG2E) + bias[half, moved(here, off), :]
            s_buf[unit % 2, moved(here, off), :] = s
            top = jnp.maximum(top, jnp.max(s, axis=0, keepdims=True))
            yield
        total = jnp.zeros((1, tok), jnp.float32)
        acc = None
        for here in tiles(half, 0, window, tok, FSTEP, cut):
            p = jnp.exp2(s_buf[unit % 2, moved(here, off), :] - top)
            total = total + jnp.sum(p, axis=0, keepdims=True)
            low = p.astype(jnp.bfloat16)
            p_of(unit, here)[...] = low
            part = dot(vt[:, here], low)
            acc = part if acc is None else acc + part
            yield
        inv = 1.0 / total
        att = (acc * inv).astype(jnp.bfloat16)
        store_heads(att_ref, att.T, rows, one, two)
        do = jnp.concatenate([do_ref[rows, one], do_ref[rows, two]], axis=0)
        scaled = (do.T.astype(jnp.float32) * inv).astype(jnp.bfloat16)
        dot_s[...] = scaled
        do_s[...] = scaled.T
        delta[...] = jnp.sum(
            scaled.astype(jnp.float32) * att.astype(jnp.float32), axis=0, keepdims=True
        )
        yield

    def back(unit):
        return backward(
            unit % 2, 0, stop, lambda here: p_of(unit, here)[...], ds_buf.at[unit % 2], *saved(unit),
            k_all, v_all, kt, dk, dv, 0, lambda dq: done(unit, dq),
        )

    together(forward(0), forward(1))
    for unit in range(2, GROUP, 2):
        together(forward(unit), back(unit - 2), forward(unit + 1), back(unit - 1))
    together(back(GROUP - 2), back(GROUP - 1))


def store_terms(terms, dk, dv, tok, base=0):
    for t, term in enumerate(terms):
        here = slice(t * tok - base, (t + 1) * tok - base)
        term[:, :HEAD] = (dk[here, :] * SCALE).astype(term.dtype)
        term[:, HEAD:] = dv[here, :].astype(term.dtype)


def attend_kernel(*refs):
    start_ref, place_ref, rx_ref, do_ref, att_ref, dq_ref, far, near2, near1, own = refs[:10]
    bias, k_all, v_all, kt, vt, q_loc, s_buf, ds_buf, dk, dv = refs[10:20]
    slots = [refs[20 + 5 * i : 25 + 5 * i] for i in range(4)]
    tok = q_loc.shape[0]

    def p_of(unit, here):
        p_buf = slots[unit % 4][0]
        return p_buf.at[moved(here, unit % 2 * tok // 2), :]

    def saved(unit):
        return slots[unit % 4][1:]

    def done(unit, dq):
        _, rows, one, two = halves(unit, tok)
        store_heads(dq_ref, (dq * SCALE).astype(jnp.bfloat16).T, rows, one, two)

    attend_body(
        None, start_ref, place_ref, rx_ref, do_ref, att_ref, bias, k_all, v_all, kt, vt,
        q_loc, s_buf, ds_buf, dk, dv, p_of, saved, done, BLOCKS * tok,
    )
    store_terms((far.at[0], far.at[1], near2, near1, own), dk, dv, tok)


def scratch(tok):
    window, reach = BLOCKS * tok, SPAN * tok + tok // 2
    bf16, f32 = jnp.bfloat16, jnp.float32
    return [
        pltpu.VMEM((2, reach, tok), f32),
        pltpu.VMEM((window, HEAD), bf16),
        pltpu.VMEM((window, HEAD), bf16),
        pltpu.VMEM((HEAD, window), bf16),
        pltpu.VMEM((HEAD, window), bf16),
        pltpu.VMEM((tok, QCOLS), bf16),
        pltpu.VMEM((2, reach, tok), f32),
        pltpu.VMEM((2, reach, tok), bf16),
        pltpu.VMEM((window, HEAD), f32),
        pltpu.VMEM((window, HEAD), f32),
    ]


def kept(tok):
    bf16 = jnp.bfloat16
    return [
        ((tok, HEAD), bf16),
        ((tok, HEAD), bf16),
        ((HEAD, tok), bf16),
        ((1, tok), jnp.float32),
    ]


def estimate(count, share, tok):
    work = count * GROUP * BLOCKS * tok * tok
    return pl.CostEstimate(
        flops=int(share * 48 * work * HEAD),
        bytes_accessed=count * 4 * 1024 * 1024,
        transcendentals=work,
    )


def attend(start, places, rx, do, first, count, at=0):
    tok = do.shape[0]
    bf16, f32 = jnp.bfloat16, jnp.float32
    wide = pl.BlockSpec((tok, QCOLS), lambda h: (0, first + h))
    cols = pl.BlockSpec((tok, KVCOLS), lambda h: (0, h))
    slot = [pltpu.VMEM((SPAN * tok + tok // 2, tok), bf16)]
    slot += [pltpu.VMEM(*a) for a in kept(tok)]
    return pl.pallas_call(
        attend_kernel,
        grid=(count,),
        in_specs=[
            pl.BlockSpec(start.shape, lambda h: (0, 0)),
            pl.BlockSpec(places.shape, lambda h: (0, 0)),
            pl.BlockSpec((*rx.shape[:2], COLS), lambda h: (0, 0, at + h)),
            pl.BlockSpec((tok, QCOLS), lambda h: (0, h)),
        ],
        out_specs=[wide, wide, pl.BlockSpec((2, tok, KVCOLS), lambda h: (0, 0, h)), cols, cols, cols],
        out_shape=[
            jax.ShapeDtypeStruct((tok, HQ * HEAD), bf16),
            jax.ShapeDtypeStruct((tok, HQ * HEAD), bf16),
            jax.ShapeDtypeStruct((2, tok, count * KVCOLS), bf16),
            jax.ShapeDtypeStruct((tok, count * KVCOLS), bf16),
            jax.ShapeDtypeStruct((tok, count * KVCOLS), bf16),
            jax.ShapeDtypeStruct((tok, count * KVCOLS), f32),
        ],
        scratch_shapes=scratch(tok) + slot * 4,
        compiler_params=pltpu.CompilerParams(vmem_limit_bytes=ATTEND_LIMIT),
        cost_estimate=estimate(count, 1.0, tok),
        name="attend",
    )(start, places, rx, do)


def attend_far_kernel(*refs):
    start_ref, place_ref, rx_ref, do_ref = refs[:4]
    att_ref, far, p_out, q_out, do_out, dot_out, delta_out, dq_out = refs[-25:-17]
    k_out, v_out, kt_out = refs[-17:-14]
    bias, k_all, v_all, kt, vt, q_loc, s_buf, ds_buf, dk, dv = refs[-14:-4]
    p_bufs = refs[-4:]
    tok = q_loc.shape[0]
    split = 2 * tok

    def p_of(unit, here):
        if here.start >= split:
            return p_out.at[unit, moved(here, split), :]
        return p_bufs[unit % 4].at[moved(here, unit % 2 * tok // 2), :]

    def saved(unit):
        return q_out.at[unit], do_out.at[unit], dot_out.at[unit], delta_out.at[unit]

    def done(unit, dq):
        dq_out[unit, :, :] = dq

    attend_body(
        split, start_ref, place_ref, rx_ref, do_ref, att_ref, bias, k_all, v_all, kt, vt,
        q_loc, s_buf, ds_buf, dk, dv, p_of, saved, done, split,
    )
    k_out[...] = k_all[split:, :]
    v_out[...] = v_all[split:, :]
    kt_out[...] = kt[:, split:]
    store_terms((far.at[0], far.at[1]), dk, dv, tok)


def attend_far(start, places, rx, do, att, first):
    tok = do.shape[0]
    count = rx.shape[2] // COLS
    near = BLOCKS * tok - 2 * tok
    bf16, f32 = jnp.bfloat16, jnp.float32
    wide = pl.BlockSpec((tok, QCOLS), lambda h: (0, first + h))
    state = [((near, tok), bf16)] + kept(tok) + [((HEAD, tok), f32)]
    state = [((GROUP, *shape), dtype) for shape, dtype in state]
    state += [((near, HEAD), bf16), ((near, HEAD), bf16), ((HEAD, near), bf16)]
    out = pl.pallas_call(
        attend_far_kernel,
        grid=(count,),
        in_specs=[
            pl.BlockSpec(start.shape, lambda h: (0, 0)),
            pl.BlockSpec(places.shape, lambda h: (0, 0)),
            pl.BlockSpec((*rx.shape[:2], COLS), lambda h: (0, 0, h)),
            pl.BlockSpec((tok, QCOLS), lambda h: (0, h)),
            pl.BlockSpec(memory_space=pl.ANY),
        ],
        out_specs=[wide, pl.BlockSpec((2, tok, KVCOLS), lambda h: (0, 0, h))]
        + [per_head(shape) for shape, _ in state],
        out_shape=[
            jax.ShapeDtypeStruct((tok, HQ * HEAD), bf16),
            jax.ShapeDtypeStruct((2, tok, count * KVCOLS), bf16),
        ]
        + [jax.ShapeDtypeStruct((count, *shape), dtype) for shape, dtype in state],
        scratch_shapes=scratch(tok) + [pltpu.VMEM((SPAN * tok + tok // 2, tok), bf16)] * 4,
        input_output_aliases={4: 0},
        compiler_params=pltpu.CompilerParams(vmem_limit_bytes=FAR_LIMIT),
        cost_estimate=estimate(count, 0.6, tok),
        name="attend_far",
    )(start, places, rx, do, att)
    return out


def per_head(shape):
    return pl.BlockSpec((None, *shape), lambda h: (h, *([0] * len(shape))))


def attend_near_kernel(*refs):
    p_in, q_in, do_in, dot_in, delta_in, dq_in, k_in, v_in, kt_in = refs[:9]
    dq_ref, near2, near1, own, dk, dv = refs[-8:-2]
    ds_bufs = refs[-2:]
    tok = near2.shape[0]
    split = 2 * tok
    dk[...] = jnp.zeros_like(dk)
    dv[...] = jnp.zeros_like(dv)

    def back(unit):
        def done(dq):
            _, rows, one, two = halves(unit, tok)
            dq = ((dq + dq_in[unit]) * SCALE).astype(jnp.bfloat16).T
            store_heads(dq_ref, dq, rows, one, two)

        return backward(
            unit % 2, split, BLOCKS * tok, lambda here: p_in[unit, moved(here, split), :],
            ds_bufs[unit % 2], q_in.at[unit], do_in.at[unit], dot_in.at[unit],
            delta_in.at[unit], k_in, v_in, kt_in, dk, dv, split, done,
        )

    for unit in range(0, GROUP, 2):
        together(back(unit), back(unit + 1))
    store_terms((near2, near1, own), dk, dv, tok)


def attend_near(state, dq, first, count, after):
    tok = dq.shape[0]
    near = BLOCKS * tok - 2 * tok
    bf16, f32 = jnp.bfloat16, jnp.float32
    wide = pl.BlockSpec((tok, QCOLS), lambda h: (0, first + h))
    cols = pl.BlockSpec((tok, KVCOLS), lambda h: (0, h))
    return pl.pallas_call(
        attend_near_kernel,
        grid=(count,),
        in_specs=[per_head(a.shape[1:]) for a in state]
        + [pl.BlockSpec(memory_space=pl.ANY)] * (1 + len(after)),
        out_specs=[wide, cols, cols, cols],
        out_shape=[
            jax.ShapeDtypeStruct((tok, HQ * HEAD), bf16),
            jax.ShapeDtypeStruct((tok, count * KVCOLS), bf16),
            jax.ShapeDtypeStruct((tok, count * KVCOLS), bf16),
            jax.ShapeDtypeStruct((tok, count * KVCOLS), f32),
        ],
        scratch_shapes=[pltpu.VMEM((near, HEAD), f32)] * 2 + [pltpu.VMEM((near, tok), bf16)] * 2,
        input_output_aliases={len(state): 0},
        compiler_params=pltpu.CompilerParams(vmem_limit_bytes=ATTEND_LIMIT),
        cost_estimate=estimate(count, 0.4, tok),
        name="attend_near",
    )(*state, dq, *after)


def split_kernel(do_ref, _, *outs):
    at = 0
    for out in outs:
        out[...] = do_ref[:, at : at + out.shape[1]]
        at += out.shape[1]


def split(do, after, counts):
    tok = do.shape[0]
    return pl.pallas_call(
        split_kernel,
        grid=(1,),
        in_specs=[pl.BlockSpec(do.shape, lambda h: (0, 0)), pl.BlockSpec(memory_space=pl.ANY)],
        out_specs=[pl.BlockSpec((tok, n * QCOLS), lambda h: (0, 0)) for n in counts],
        out_shape=[jax.ShapeDtypeStruct((tok, n * QCOLS), jnp.bfloat16) for n in counts],
        compiler_params=pltpu.CompilerParams(vmem_limit_bytes=VMEM_LIMIT),
        name="split",
    )(do, after)


def added(near, far):
    return (near[...].astype(jnp.float32) + far.astype(jnp.float32)).astype(jnp.bfloat16)


def near1_kernel(near1, far, *rest):
    out1 = rest[-1]
    out1[...] = added(near1, far[1])


def near2_kernel(near2, far, out2):
    out2[...] = added(near2, far[0])


def last_near2_kernel(near2, far, _, out2):
    out2[...] = added(near2, far[0])


def merge(kernel, outs, *args):
    return pl.pallas_call(
        kernel,
        out_shape=[jax.ShapeDtypeStruct(a.shape, a.dtype) for a in outs],
        compiler_params=pltpu.CompilerParams(vmem_limit_bytes=SMALL_LIMIT),
        name="merge",
    )(*args)


def finish_kernel(own_a, back2_a, back1_a, own_b, back2_b, back1_b, gk_ref, gv_ref):
    width = own_a.shape[1]
    a, b = (own_a, back2_a, back1_a), (own_b, back2_b, back1_b)
    for at, (own, back2, back1) in ((0, a), (width, b)):
        total = own[...] + back2[...].astype(jnp.float32) + back1[...].astype(jnp.float32)
        for i in range(own.shape[1] // KVCOLS):
            cols = slice((at // KVCOLS + i) * HEAD, (at // KVCOLS + i + 1) * HEAD)
            mid = i * KVCOLS + HEAD
            gk_ref[:, cols] = total[:, mid - HEAD : mid].astype(jnp.bfloat16)
            gv_ref[:, cols] = total[:, mid : mid + HEAD].astype(jnp.bfloat16)


def finish(*parts):
    tok = parts[0].shape[0]
    return pl.pallas_call(
        finish_kernel,
        out_shape=[jax.ShapeDtypeStruct((tok, KV_HEADS * HEAD), jnp.bfloat16)] * 2,
        compiler_params=pltpu.CompilerParams(vmem_limit_bytes=SMALL_LIMIT),
        name="finish",
    )(*parts)


def body(queries, keys, values, d_out, doc_ids, send_order, place):
    tok = queries.shape[0]
    shard = lax.axis_index("ctx")
    sent = []
    for first, count in CHUNKS:
        if first == 0:
            later = (doc_ids, place)
            packed, doc_ids, place = pack(send_order, queries, keys, values, first, count, later)
        else:
            packed = pack(send_order, queries, keys, values, first, count)
        sent.append(lax.all_to_all(packed, ("dp", "ctx"), split_axis=0, concat_axis=0, tiled=True))

    places = jnp.concatenate([shifted(place, SPAN - t) for t in range(SPAN)] + [place], axis=0)
    docs = jnp.pad(doc_ids[0], (SPAN * tok, 0), constant_values=-1)
    docs = lax.dynamic_slice_in_dim(docs, shard * tok, BLOCKS * tok, 0)
    before = docs[:, None] < docs[None, SPAN * tok :]
    start = jnp.sum(before.astype(jnp.int32), axis=0)[None, :]

    (first_a, count_a), (first_b, count_b) = CHUNKS
    do_a, do_b = split(d_out[0], doc_ids, (count_a, count_b))
    att, dq, far_a, near2_a, near1_a, own_a = attend(start, places, sent[0], do_a, first_a, count_a)
    far_a = shifted(far_a, -2)
    att, far_b, *state = attend_far(start, places, sent[1], do_b, att, first_b)
    far_b = shifted(far_b, -2)
    (back1_a,) = merge(near1_kernel, (near1_a,), near1_a, far_a)
    (back2_a,) = merge(near2_kernel, (near2_a,), near2_a, far_a)
    back1_a, back2_a = shifted(back1_a, -1), shifted(back2_a, -2)
    dq, near2_b, near1_b, own_b = attend_near(state, dq, first_b, count_b, ())
    (back1_b,) = merge(near1_kernel, (near1_b,), near1_b, far_b, back1_a)
    (back2_b,) = merge(last_near2_kernel, (near2_b,), near2_b, far_b, back1_b)
    back1_b, back2_b = shifted(back1_b, -1), shifted(back2_b, -2)
    grad_k, grad_v = finish(own_a, back2_a, back1_a, own_b, back2_b, back1_b)
    return att[None], dq[None], grad_k[None], grad_v[None]


def solution(mesh):
    in_specs = (
        P(("dp", "ctx"), None),
        P(("dp", "ctx"), None),
        P(("dp", "ctx"), None),
        P("dp", "ctx", None),
        P("dp", None),
        P(("dp", "ctx"), None),
        P(("dp", "ctx"), None),
    )
    out_specs = (P("dp", "ctx", None),) * 4
    return jax.shard_map(body, mesh=mesh, in_specs=in_specs, out_specs=out_specs, check_vma=False)
```

```python
import functools
import math

import jax
import jax.numpy as jnp
from jax import lax
from jax.experimental import pallas as pl
from jax.experimental.pallas import tpu as pltpu
from jax.sharding import PartitionSpec as P

HQ = 32
KV_HEADS = 4
N_DP = 4
GROUP = HQ // KV_HEADS
HEAD = 128
SPAN = 4
BLOCKS = SPAN + 1
QCOLS = GROUP * HEAD
KVCOLS = 2 * HEAD
COLS = QCOLS + BLOCKS * KVCOLS
FSTEP = 512
BSTEP = 600
CHUNKS = ((0, 2), (2, 2))
SCALE = 1.0 / math.sqrt(HEAD)
LOG2E = math.log2(math.e)
MASKED = -1e30
VMEM_LIMIT = 60 * 1024 * 1024
ATTEND_LIMIT = 32 * 1024 * 1024
FAR_LIMIT = 32 * 1024 * 1024
SMALL_LIMIT = 8 * 1024 * 1024
SPLIT_LIMIT = 16 * 1024 * 1024


def dot(a, b):
    return jnp.dot(a, b, preferred_element_type=jnp.float32)


def shifted(block, distance):
    devices = range(lax.axis_size("ctx"))
    route = [(i - distance, i) for i in devices if i - distance in devices]
    return lax.ppermute(block, "ctx", route)


def pack_kernel(order_ref, q_ref, k_ref, v_ref, *rest):
    out_ref = rest[-1]
    tok = q_ref.shape[0]
    n, grain, _ = out_ref.shape
    order = jnp.broadcast_to(order_ref[...].astype(jnp.float32), (tok, tok)).T
    column = lax.broadcasted_iota(jnp.int32, (tok, tok), 1)
    onehot = (order.astype(jnp.int32) == column).astype(jnp.bfloat16)
    q = dot(onehot, q_ref[...]).astype(jnp.bfloat16)
    out_ref[:, :, :QCOLS] = q.reshape(n, grain, QCOLS)
    kv = jnp.concatenate([k_ref[...], v_ref[...]], axis=1)
    kv = dot(onehot, kv).astype(jnp.bfloat16).reshape(n, grain, KVCOLS)
    ctx = n // N_DP
    for t in range(BLOCKS):
        back = SPAN - t
        at = QCOLS + t * KVCOLS
        for p in range(N_DP):
            if back:
                none = jnp.zeros((back, grain, KVCOLS), jnp.bfloat16)
                out_ref[p * ctx : p * ctx + back, :, at : at + KVCOLS] = none
            out_ref[p * ctx + back : (p + 1) * ctx, :, at : at + KVCOLS] = kv[
                p * ctx : (p + 1) * ctx - back
            ]


def first_pack_kernel(order_ref, q_ref, k_ref, v_ref, doc_ref, place_ref, out_ref, doc_out, place_out):
    doc_out[...] = doc_ref[...]
    place_out[...] = place_ref[...]
    pack_kernel(order_ref, q_ref, k_ref, v_ref, out_ref)


def pack(order, queries, keys, values, first, count, later=()):
    tok = queries.shape[0]
    devices = lax.axis_size("dp") * lax.axis_size("ctx")
    grain = tok // devices
    whole = [pl.BlockSpec(a.shape, lambda h: (0, 0)) for a in later]
    out = pl.pallas_call(
        first_pack_kernel if later else pack_kernel,
        grid=(count,),
        in_specs=[
            pl.BlockSpec(order.shape, lambda h: (0, 0)),
            pl.BlockSpec((tok, QCOLS), lambda h: (0, first + h)),
            pl.BlockSpec((tok, HEAD), lambda h: (0, first + h)),
            pl.BlockSpec((tok, HEAD), lambda h: (0, first + h)),
        ]
        + whole,
        out_specs=[pl.BlockSpec((devices, grain, COLS), lambda h: (0, 0, h))] + whole,
        out_shape=[jax.ShapeDtypeStruct((devices, grain, count * COLS), jnp.bfloat16)]
        + [jax.ShapeDtypeStruct(a.shape, a.dtype) for a in later],
        compiler_params=pltpu.CompilerParams(vmem_limit_bytes=VMEM_LIMIT),
        name="pack",
    )(order, queries, keys, values, *later)
    return out if later else out[0]


def tiles(half, low, high, tok, step, cut=None):
    low = max(low, half * tok // 2)
    high = min(high, SPAN * tok + (half + 1) * tok // 2)
    for low, high in ((low, high),) if cut is None else ((low, cut), (cut, high)):
        size = (high - low) // pl.cdiv(high - low, step)
        for i in range(low, high, size):
            yield slice(i, i + size)


def moved(here, base):
    return slice(here.start - base, here.stop - base)


def together(*work):
    work = list(work)
    while work:
        work = [w for w in work if next(w, work) is None]


def halves(unit, tok):
    half, pair = unit % 2, unit // 2
    rows = slice(half * tok // 2, (half + 1) * tok // 2)
    one, two = ((2 * pair + i) * HEAD for i in range(2))
    return half, rows, slice(one, one + HEAD), slice(two, two + HEAD)


def backward(half, low, high, p_of, ds_buf, q, do_s, dot_s, delta, k_all, v_all, kt, dk, dv, base, done):
    tok = q.shape[0]
    spans = list(tiles(half, low, high, tok, BSTEP))
    for here in spans:
        p = p_of(here)
        dp = dot(v_all[moved(here, base), :], dot_s[...])
        ds = (p.astype(jnp.float32) * (dp - delta[...])).astype(jnp.bfloat16)
        ds_buf[moved(here, spans[0].start), :] = ds
        yield
        dv[moved(here, base), :] += dot(p, do_s[...])
        dk[moved(here, base), :] += dot(ds, q[...])
        yield
    first, last = spans[0].start, spans[-1].stop
    done(dot(kt[:, first - base : last - base], ds_buf[: last - first, :]))
    yield


def store_heads(ref, value, rows, one, two):
    half = value.shape[0] // 2
    ref[rows, one] = value[:half]
    ref[rows, two] = value[half:]


def attend_body(
    cut, start_ref, place_ref, rx_ref, do_ref, att_ref, bias, k_all, v_all, kt, vt,
    q_loc, s_buf, ds_buf, dk, dv, p_of, saved, done, stop,
):
    tok = q_loc.shape[0]
    window = BLOCKS * tok
    reach = SPAN * tok + tok // 2

    @pl.when(pl.program_id(0) == 0)
    def _():
        u = lax.broadcasted_iota(jnp.int32, (reach, tok // 2), 0)
        t = lax.broadcasted_iota(jnp.int32, (reach, tok // 2), 1)
        for half in range(2):
            off = half * tok // 2
            start = start_ref[:, off : off + tok // 2] - off
            keep = (u >= start) & (u <= t + SPAN * tok)
            add = jnp.where(keep, 0.0, MASKED)
            bias[half, :, : tok // 2] = add
            bias[half, :, tok // 2 :] = add

    row = lax.broadcasted_iota(jnp.int32, (tok, tok), 0)
    rx = rx_ref[...].reshape(tok, COLS)
    for t in range(BLOCKS):
        spread = (place_ref[t : t + 1, :] == row).astype(jnp.bfloat16)
        at = QCOLS + t * KVCOLS
        kv = dot(spread, rx[:, at : at + KVCOLS])
        here = slice(t * tok, (t + 1) * tok)
        k_all[here, :] = kv[:, :HEAD].astype(jnp.bfloat16)
        v_all[here, :] = kv[:, HEAD:].astype(jnp.bfloat16)
        kt[:, here] = kv[:, :HEAD].T.astype(jnp.bfloat16)
        vt[:, here] = kv[:, HEAD:].T.astype(jnp.bfloat16)
        if t == SPAN:
            q_loc[...] = dot(spread, rx[:, :QCOLS]).astype(jnp.bfloat16)
    dk[...] = jnp.zeros_like(dk)
    dv[...] = jnp.zeros_like(dv)

    def forward(unit):
        half, rows, one, two = halves(unit, tok)
        off = half * tok // 2
        q_u, do_s, dot_s, delta = saved(unit)
        q = jnp.concatenate([q_loc[rows, one], q_loc[rows, two]], axis=0)
        q_u[...] = q
        qt = q.T
        top = jnp.full((1, tok), MASKED, jnp.float32)
        for here in tiles(half, 0, window, tok, FSTEP, cut):
            s = dot(k_all[here, :], qt) * (SCALE * LOG2E) + bias[half, moved(here, off), :]
            s_buf[unit % 2, moved(here, off), :] = s
            top = jnp.maximum(top, jnp.max(s, axis=0, keepdims=True))
            yield
        total = jnp.zeros((1, tok), jnp.float32)
        acc = None
        for here in tiles(half, 0, window, tok, FSTEP, cut):
            p = jnp.exp2(s_buf[unit % 2, moved(here, off), :] - top)
            total = total + jnp.sum(p, axis=0, keepdims=True)
            low = p.astype(jnp.bfloat16)
            p_of(unit, here)[...] = low
            part = dot(vt[:, here], low)
            acc = part if acc is None else acc + part
            yield
        inv = 1.0 / total
        att = (acc * inv).astype(jnp.bfloat16)
        store_heads(att_ref, att.T, rows, one, two)
        do = jnp.concatenate([do_ref[rows, one], do_ref[rows, two]], axis=0)
        scaled = (do.T.astype(jnp.float32) * inv).astype(jnp.bfloat16)
        dot_s[...] = scaled
        do_s[...] = scaled.T
        delta[...] = jnp.sum(
            scaled.astype(jnp.float32) * att.astype(jnp.float32), axis=0, keepdims=True
        )
        yield

    def back(unit):
        return backward(
            unit % 2, 0, stop, lambda here: p_of(unit, here)[...], ds_buf.at[unit % 2], *saved(unit),
            k_all, v_all, kt, dk, dv, 0, lambda dq: done(unit, dq),
        )

    together(forward(0), forward(1))
    for unit in range(2, GROUP, 2):
        together(forward(unit), back(unit - 2), forward(unit + 1), back(unit - 1))
    together(back(GROUP - 2), back(GROUP - 1))


def store_terms(terms, dk, dv, tok, base=0):
    for t, term in enumerate(terms):
        here = slice(t * tok - base, (t + 1) * tok - base)
        term[:, :HEAD] = (dk[here, :] * SCALE).astype(term.dtype)
        term[:, HEAD:] = dv[here, :].astype(term.dtype)


def attend_kernel(*refs):
    start_ref, place_ref, rx_ref, do_ref, att_ref, dq_ref, far, near2, near1, own = refs[:10]
    bias, k_all, v_all, kt, vt, q_loc, s_buf, ds_buf, dk, dv = refs[10:20]
    slots = [refs[20 + 5 * i : 25 + 5 * i] for i in range(4)]
    tok = q_loc.shape[0]

    def p_of(unit, here):
        p_buf = slots[unit % 4][0]
        return p_buf.at[moved(here, unit % 2 * tok // 2), :]

    def saved(unit):
        return slots[unit % 4][1:]

    def done(unit, dq):
        _, rows, one, two = halves(unit, tok)
        store_heads(dq_ref, (dq * SCALE).astype(jnp.bfloat16).T, rows, one, two)

    attend_body(
        None, start_ref, place_ref, rx_ref, do_ref, att_ref, bias, k_all, v_all, kt, vt,
        q_loc, s_buf, ds_buf, dk, dv, p_of, saved, done, BLOCKS * tok,
    )
    store_terms((far.at[0], far.at[1], near2, near1, own), dk, dv, tok)


def scratch(tok):
    window, reach = BLOCKS * tok, SPAN * tok + tok // 2
    bf16, f32 = jnp.bfloat16, jnp.float32
    return [
        pltpu.VMEM((2, reach, tok), f32),
        pltpu.VMEM((window, HEAD), bf16),
        pltpu.VMEM((window, HEAD), bf16),
        pltpu.VMEM((HEAD, window), bf16),
        pltpu.VMEM((HEAD, window), bf16),
        pltpu.VMEM((tok, QCOLS), bf16),
        pltpu.VMEM((2, reach, tok), f32),
        pltpu.VMEM((2, reach, tok), bf16),
        pltpu.VMEM((window, HEAD), f32),
        pltpu.VMEM((window, HEAD), f32),
    ]


def kept(tok):
    bf16 = jnp.bfloat16
    return [
        ((tok, HEAD), bf16),
        ((tok, HEAD), bf16),
        ((HEAD, tok), bf16),
        ((1, tok), jnp.float32),
    ]


def estimate(count, share, tok):
    work = count * GROUP * BLOCKS * tok * tok
    return pl.CostEstimate(
        flops=int(share * 48 * work * HEAD),
        bytes_accessed=count * 4 * 1024 * 1024,
        transcendentals=work,
    )


def attend(start, places, rx, do, first, count, at=0):
    tok = do.shape[0]
    bf16, f32 = jnp.bfloat16, jnp.float32
    wide = pl.BlockSpec((tok, QCOLS), lambda h: (0, first + h))
    cols = pl.BlockSpec((tok, KVCOLS), lambda h: (0, h))
    slot = [pltpu.VMEM((SPAN * tok + tok // 2, tok), bf16)]
    slot += [pltpu.VMEM(*a) for a in kept(tok)]
    return pl.pallas_call(
        attend_kernel,
        grid=(count,),
        in_specs=[
            pl.BlockSpec(start.shape, lambda h: (0, 0)),
            pl.BlockSpec(places.shape, lambda h: (0, 0)),
            pl.BlockSpec((*rx.shape[:2], COLS), lambda h: (0, 0, at + h)),
            pl.BlockSpec((tok, QCOLS), lambda h: (0, h)),
        ],
        out_specs=[wide, wide, pl.BlockSpec((2, tok, KVCOLS), lambda h: (0, 0, h)), cols, cols, cols],
        out_shape=[
            jax.ShapeDtypeStruct((tok, HQ * HEAD), bf16),
            jax.ShapeDtypeStruct((tok, HQ * HEAD), bf16),
            jax.ShapeDtypeStruct((2, tok, count * KVCOLS), bf16),
            jax.ShapeDtypeStruct((tok, count * KVCOLS), bf16),
            jax.ShapeDtypeStruct((tok, count * KVCOLS), bf16),
            jax.ShapeDtypeStruct((tok, count * KVCOLS), f32),
        ],
        scratch_shapes=scratch(tok) + slot * 4,
        compiler_params=pltpu.CompilerParams(vmem_limit_bytes=ATTEND_LIMIT),
        cost_estimate=estimate(count, 1.0, tok),
        name="attend",
    )(start, places, rx, do)


def attend_far_kernel(*refs):
    start_ref, place_ref, rx_ref, do_ref = refs[:4]
    att_ref, far, p_out, q_out, do_out, dot_out, delta_out, dq_out = refs[-25:-17]
    k_out, v_out, kt_out = refs[-17:-14]
    bias, k_all, v_all, kt, vt, q_loc, s_buf, ds_buf, dk, dv = refs[-14:-4]
    p_bufs = refs[-4:]
    tok = q_loc.shape[0]
    split = 2 * tok

    def p_of(unit, here):
        if here.start >= split:
            return p_out.at[unit, moved(here, split), :]
        return p_bufs[unit % 4].at[moved(here, unit % 2 * tok // 2), :]

    def saved(unit):
        return q_out.at[unit], do_out.at[unit], dot_out.at[unit], delta_out.at[unit]

    def done(unit, dq):
        dq_out[unit, :, :] = dq

    attend_body(
        split, start_ref, place_ref, rx_ref, do_ref, att_ref, bias, k_all, v_all, kt, vt,
        q_loc, s_buf, ds_buf, dk, dv, p_of, saved, done, split,
    )
    k_out[...] = k_all[split:, :]
    v_out[...] = v_all[split:, :]
    kt_out[...] = kt[:, split:]
    store_terms((far.at[0], far.at[1]), dk, dv, tok)


def attend_far(start, places, rx, do, att, first):
    tok = do.shape[0]
    count = rx.shape[2] // COLS
    near = BLOCKS * tok - 2 * tok
    bf16, f32 = jnp.bfloat16, jnp.float32
    wide = pl.BlockSpec((tok, QCOLS), lambda h: (0, first + h))
    state = [((near, tok), bf16)] + kept(tok) + [((HEAD, tok), f32)]
    state = [((GROUP, *shape), dtype) for shape, dtype in state]
    state += [((near, HEAD), bf16), ((near, HEAD), bf16), ((HEAD, near), bf16)]
    out = pl.pallas_call(
        attend_far_kernel,
        grid=(count,),
        in_specs=[
            pl.BlockSpec(start.shape, lambda h: (0, 0)),
            pl.BlockSpec(places.shape, lambda h: (0, 0)),
            pl.BlockSpec((*rx.shape[:2], COLS), lambda h: (0, 0, h)),
            pl.BlockSpec((tok, QCOLS), lambda h: (0, h)),
            pl.BlockSpec(memory_space=pl.ANY),
        ],
        out_specs=[wide, pl.BlockSpec((2, tok, KVCOLS), lambda h: (0, 0, h))]
        + [per_head(shape) for shape, _ in state],
        out_shape=[
            jax.ShapeDtypeStruct((tok, HQ * HEAD), bf16),
            jax.ShapeDtypeStruct((2, tok, count * KVCOLS), bf16),
        ]
        + [jax.ShapeDtypeStruct((count, *shape), dtype) for shape, dtype in state],
        scratch_shapes=scratch(tok) + [pltpu.VMEM((SPAN * tok + tok // 2, tok), bf16)] * 4,
        input_output_aliases={4: 0},
        compiler_params=pltpu.CompilerParams(vmem_limit_bytes=FAR_LIMIT),
        cost_estimate=estimate(count, 0.6, tok),
        name="attend_far",
    )(start, places, rx, do, att)
    return out


def per_head(shape):
    return pl.BlockSpec((None, *shape), lambda h: (h, *([0] * len(shape))))


def attend_near_kernel(*refs):
    p_in, q_in, do_in, dot_in, delta_in, dq_in, k_in, v_in, kt_in = refs[:9]
    dq_ref, near2, near1, own, dk, dv = refs[-8:-2]
    ds_bufs = refs[-2:]
    tok = near2.shape[0]
    split = 2 * tok
    dk[...] = jnp.zeros_like(dk)
    dv[...] = jnp.zeros_like(dv)

    def back(unit):
        def done(dq):
            _, rows, one, two = halves(unit, tok)
            dq = ((dq + dq_in[unit]) * SCALE).astype(jnp.bfloat16).T
            store_heads(dq_ref, dq, rows, one, two)

        return backward(
            unit % 2, split, BLOCKS * tok, lambda here: p_in[unit, moved(here, split), :],
            ds_bufs[unit % 2], q_in.at[unit], do_in.at[unit], dot_in.at[unit],
            delta_in.at[unit], k_in, v_in, kt_in, dk, dv, split, done,
        )

    for unit in range(0, GROUP, 2):
        together(back(unit), back(unit + 1))
    store_terms((near2, near1, own), dk, dv, tok)


def attend_near(state, dq, first, count, after):
    tok = dq.shape[0]
    near = BLOCKS * tok - 2 * tok
    bf16, f32 = jnp.bfloat16, jnp.float32
    wide = pl.BlockSpec((tok, QCOLS), lambda h: (0, first + h))
    cols = pl.BlockSpec((tok, KVCOLS), lambda h: (0, h))
    return pl.pallas_call(
        attend_near_kernel,
        grid=(count,),
        in_specs=[per_head(a.shape[1:]) for a in state]
        + [pl.BlockSpec(memory_space=pl.ANY)] * (1 + len(after)),
        out_specs=[wide, cols, cols, cols],
        out_shape=[
            jax.ShapeDtypeStruct((tok, HQ * HEAD), bf16),
            jax.ShapeDtypeStruct((tok, count * KVCOLS), bf16),
            jax.ShapeDtypeStruct((tok, count * KVCOLS), bf16),
            jax.ShapeDtypeStruct((tok, count * KVCOLS), f32),
        ],
        scratch_shapes=[pltpu.VMEM((near, HEAD), f32)] * 2 + [pltpu.VMEM((near, tok), bf16)] * 2,
        input_output_aliases={len(state): 0},
        compiler_params=pltpu.CompilerParams(vmem_limit_bytes=ATTEND_LIMIT),
        cost_estimate=estimate(count, 0.4, tok),
        name="attend_near",
    )(*state, dq, *after)


def split_kernel(do_ref, _, *outs):
    at = 0
    for out in outs:
        out[...] = do_ref[:, at : at + out.shape[1]]
        at += out.shape[1]


def split(do, after, counts):
    tok = do.shape[0]
    return pl.pallas_call(
        split_kernel,
        grid=(1,),
        in_specs=[pl.BlockSpec(do.shape, lambda h: (0, 0)), pl.BlockSpec(memory_space=pl.ANY)],
        out_specs=[pl.BlockSpec((tok, n * QCOLS), lambda h: (0, 0)) for n in counts],
        out_shape=[jax.ShapeDtypeStruct((tok, n * QCOLS), jnp.bfloat16) for n in counts],
        compiler_params=pltpu.CompilerParams(vmem_limit_bytes=SPLIT_LIMIT),
        name="split",
    )(do, after)


def added(near, far):
    return (near[...].astype(jnp.float32) + far.astype(jnp.float32)).astype(jnp.bfloat16)


def near1_kernel(near1, far, *rest):
    out1 = rest[-1]
    out1[...] = added(near1, far[1])


def near2_kernel(near2, far, out2):
    out2[...] = added(near2, far[0])


def last_near2_kernel(near2, far, _, out2):
    out2[...] = added(near2, far[0])


def merge(kernel, outs, *args):
    return pl.pallas_call(
        kernel,
        out_shape=[jax.ShapeDtypeStruct(a.shape, a.dtype) for a in outs],
        compiler_params=pltpu.CompilerParams(vmem_limit_bytes=SMALL_LIMIT),
        name="merge",
    )(*args)


def finish_kernel(own_a, back2_a, back1_a, own_b, back2_b, back1_b, gk_ref, gv_ref):
    width = own_a.shape[1]
    a, b = (own_a, back2_a, back1_a), (own_b, back2_b, back1_b)
    for at, (own, back2, back1) in ((0, a), (width, b)):
        total = own[...] + back2[...].astype(jnp.float32) + back1[...].astype(jnp.float32)
        for i in range(own.shape[1] // KVCOLS):
            cols = slice((at // KVCOLS + i) * HEAD, (at // KVCOLS + i + 1) * HEAD)
            mid = i * KVCOLS + HEAD
            gk_ref[:, cols] = total[:, mid - HEAD : mid].astype(jnp.bfloat16)
            gv_ref[:, cols] = total[:, mid : mid + HEAD].astype(jnp.bfloat16)


def finish(*parts):
    tok = parts[0].shape[0]
    return pl.pallas_call(
        finish_kernel,
        out_shape=[jax.ShapeDtypeStruct((tok, KV_HEADS * HEAD), jnp.bfloat16)] * 2,
        compiler_params=pltpu.CompilerParams(vmem_limit_bytes=SMALL_LIMIT),
        name="finish",
    )(*parts)


def body(queries, keys, values, d_out, doc_ids, send_order, place):
    tok = queries.shape[0]
    shard = lax.axis_index("ctx")
    sent = []
    for first, count in CHUNKS:
        if first == 0:
            later = (doc_ids, place)
            packed, doc_ids, place = pack(send_order, queries, keys, values, first, count, later)
        else:
            packed = pack(send_order, queries, keys, values, first, count)
        sent.append(lax.all_to_all(packed, ("dp", "ctx"), split_axis=0, concat_axis=0, tiled=True))

    places = jnp.concatenate([shifted(place, SPAN - t) for t in range(SPAN)] + [place], axis=0)
    docs = jnp.pad(doc_ids[0], (SPAN * tok, 0), constant_values=-1)
    docs = lax.dynamic_slice_in_dim(docs, shard * tok, BLOCKS * tok, 0)
    before = docs[:, None] < docs[None, SPAN * tok :]
    start = jnp.sum(before.astype(jnp.int32), axis=0)[None, :]

    (first_a, count_a), (first_b, count_b) = CHUNKS
    do_a, do_b = split(d_out[0], doc_ids, (count_a, count_b))
    att, dq, far_a, near2_a, near1_a, own_a = attend(start, places, sent[0], do_a, first_a, count_a)
    far_a = shifted(far_a, -2)
    att, far_b, *state = attend_far(start, places, sent[1], do_b, att, first_b)
    far_b = shifted(far_b, -2)
    (back1_a,) = merge(near1_kernel, (near1_a,), near1_a, far_a)
    (back2_a,) = merge(near2_kernel, (near2_a,), near2_a, far_a)
    back1_a, back2_a = shifted(back1_a, -1), shifted(back2_a, -2)
    dq, near2_b, near1_b, own_b = attend_near(state, dq, first_b, count_b, ())
    (back1_b,) = merge(near1_kernel, (near1_b,), near1_b, far_b, back1_a)
    (back2_b,) = merge(last_near2_kernel, (near2_b,), near2_b, far_b, back1_b)
    back1_b, back2_b = shifted(back1_b, -1), shifted(back2_b, -2)
    grad_k, grad_v = finish(own_a, back2_a, back1_a, own_b, back2_b, back1_b)
    return att[None], dq[None], grad_k[None], grad_v[None]


def solution(mesh):
    in_specs = (
        P(("dp", "ctx"), None),
        P(("dp", "ctx"), None),
        P(("dp", "ctx"), None),
        P("dp", "ctx", None),
        P("dp", None),
        P(("dp", "ctx"), None),
        P(("dp", "ctx"), None),
    )
    out_specs = (P("dp", "ctx", None),) * 4
    return jax.shard_map(body, mesh=mesh, in_specs=in_specs, out_specs=out_specs, check_vma=False)
```
